512 devices in a mesh: slab: 64 (over z, x_lo, core), mode: 8 (over x_hi, y).
Axes of the slice: x: 4 (x_hi: 2, x_lo: 2; x = x_hi * 2 + x_lo), y: 4, z: 16, core: 2. Of those that a mesh axis runs over, the one named last changes fastest.
Arguments:
- initial_block: bfloat16 [96, 64, 64, 128], P('mode', 'slab'), may hold values from -180 to 180
- labels: int32 [64, 64, 128], P('slab'), may hold values from 0 to 3
- filter_low: float32 [], replicated, may hold values from 1 to 3
- filter_high: float32 [], replicated, may hold values from 22 to 24
Outputs:
- modes_out: bfloat16 [96, 64, 64, 128], P('mode', 'slab')
- projected: float32 [96, 96], replicated
The draws below stay inside these ranges and needn't reach their ends.
Inputs may be any that keep to these rules, and one draw needn't show every extreme that they name: `labels`: 0 marks a voxel outside the brain; 1, 2 and 3 are tissue classes.
All inputs are finite; a program needn't handle non-finite values.
Results may differ from the reference program's by a relative error of at most 0.0015.
The reference program's roundings to bfloat16 on the way (of `filtered`, `applied` and `rotation`) count: a program that leaves them out, or rounds other values in their place, can miss the bound.
Values may be sent and summed in bfloat16 or wider, within the bound.
No kernel may reach another device: no remote copies, remote signals or barrier semaphores. Data moves between devices by JAX's collectives and lax.ppermute only.
A program may use at most 64 MiB of HBM per device.

```python
import math
import jax
import jax.numpy as jnp
from jax import lax

MODES = 96
DEGREE = 4
NX = 128
NY = 64
NZ = 64
CELLS = 524288


def draw_initial_block(key, part):
    key_values = jax.random.fold_in(key, 11)
    key_modes = jax.random.fold_in(key, 23)
    depth = jnp.arange(NZ, dtype=jnp.float32) / max(NZ - 1, 1)
    mode_scale = jnp.exp(jax.random.uniform(key_modes, (MODES,), jnp.float32, 0.0, math.log(10.0)))
    values = jnp.clip(jax.random.normal(key_values, (MODES, NZ, NY, NX), jnp.float32), -6.0, 6.0)
    profile = 1.0 + 2.0 * depth
    whole = values * profile[None, :, None, None] * mode_scale[:, None, None, None]
    return whole.astype(jnp.bfloat16)


def set_ends(values, rng, smallest, high):
    shape = values.shape
    place = [jax.random.randint(jax.random.fold_in(rng, axis), (), 0, shape[axis]) for axis in range(len(shape))]
    values = values.at[tuple(place)].set(smallest)
    longest = shape.index(max(shape))
    place[longest] = (place[longest] + 1) % shape[longest]
    return values.at[tuple(place)].set(high)


def setup_inputs(seed: int = 0) -> dict:
    splits = jax.random.split(jax.random.key(seed), 5)
    initial_block = draw_initial_block(jax.random.fold_in(splits[4], 71), 0)
    labels = set_ends(jax.random.randint(splits[1], (NZ, NY, NX), 0, 4), jax.random.fold_in(splits[1], 1), 0, 3).astype(jnp.int32)
    filter_low = jnp.clip(jax.random.uniform(splits[2], (), jnp.float32, 1.0, 3.0), 1.0, 3.0)
    filter_high = jnp.clip(jax.random.uniform(splits[3], (), jnp.float32, 22.0, 24.0), 22.0, 24.0)
    return {"initial_block": initial_block, "labels": labels, "filter_low": filter_low, "filter_high": filter_high}


ROOTS = (0.0, 0.7745967, 1.0, 1.3416408)

def strength_of(labels):
    total = jnp.zeros(labels.shape, jnp.float32)
    for level in range(1, 4):
        total = total + jnp.where(labels == level, ROOTS[level], 0.0)
    return total

def face_weights(strong, padded):
    return (strong * padded[:-2, 1:-1, 1:-1], strong * padded[2:, 1:-1, 1:-1], strong * padded[1:-1, :-2, 1:-1], strong * padded[1:-1, 2:, 1:-1], strong * padded[1:-1, 1:-1, :-2], strong * padded[1:-1, 1:-1, 2:])

def combine_faces(field, padded, weights):
    beside_all = (padded[:, :-2, 1:-1, 1:-1], padded[:, 2:, 1:-1, 1:-1], padded[:, 1:-1, :-2, 1:-1], padded[:, 1:-1, 2:, 1:-1], padded[:, 1:-1, 1:-1, :-2], padded[:, 1:-1, 1:-1, 2:])
    total = weights[0] * (field - beside_all[0])
    for weight, other in zip(weights[1:], beside_all[1:]):
        total = total + weight * (field - other)
    return total

def chebyshev(block, apply_fn, low, high):
    centre = 0.5 * (high + low)
    half = 0.5 * (high - low)
    prev = block
    cur = (apply_fn(block) - centre * block) / half
    for step in range(DEGREE - 1):
        nxt = 2.0 * (apply_fn(cur) - centre * cur) / half - prev
        prev, cur = (cur, nxt)
    return cur

def reference(initial_block, labels, filter_low, filter_high):
    strong = strength_of(labels)
    mask = (labels > 0).astype(jnp.float32)
    weights = face_weights(strong, jnp.pad(strong, 1))

    def apply_fn(field):
        return combine_faces(field, jnp.pad(field, ((0, 0), (1, 1), (1, 1), (1, 1))), weights)

    def one_mode(single):
        block = single.astype(jnp.float32)[None] * mask[None]
        cur = chebyshev(block, apply_fn, filter_low, filter_high)
        image = apply_fn(cur)
        return (cur[0].astype(jnp.bfloat16), image[0].astype(jnp.bfloat16))
    filtered, applied = lax.map(one_mode, initial_block)
    flat = filtered.reshape(MODES, -1)
    flat_applied = applied.reshape(MODES, -1)
    gram = jnp.einsum('mc,nc->mn', flat.astype(jnp.float32), flat.astype(jnp.float32), preferred_element_type=jnp.float32)
    cross = jnp.einsum('mc,nc->mn', flat.astype(jnp.float32), flat_applied.astype(jnp.float32), preferred_element_type=jnp.float32)
    lower = jnp.linalg.cholesky(gram)
    inverse = jax.scipy.linalg.solve_triangular(lower, jnp.eye(MODES, dtype=jnp.float32), lower=True)
    projected = jnp.dot(jnp.dot(inverse, cross, precision=lax.Precision.HIGHEST), inverse.T, precision=lax.Precision.HIGHEST)
    rotation = inverse.T.astype(jnp.bfloat16)
    scale = math.sqrt(CELLS)
    turned = jnp.einsum('mj,mc->jc', rotation.astype(jnp.float32), flat.astype(jnp.float32), preferred_element_type=jnp.float32)
    modes_out = (turned * scale).astype(jnp.bfloat16).reshape(MODES, NZ, NY, NX)
    return (modes_out, projected)
```

```python
import functools
import math

import jax
import jax.numpy as jnp
from jax import lax
from jax.experimental import pallas as pl
from jax.experimental.pallas import tpu as pltpu
from jax.sharding import Mesh, PartitionSpec as P

DEGREE = 4
ROOTS = (0.0, 0.7745967, 1.0, 1.3416408)
REACH = DEGREE + 1

AXES = ("z", "xl", "core", "xh", "y")
GROUP = ("xl", "core")
MODE = ("xh", "y")
LAYER = ("xh", "y", "xl", "core")


def filter_kernel(bounds, far_lo, lo, own, hi, far_hi, out, even, odd, weak_even, weak_odd, strong, degree):
    planes, height, width = strong.shape
    local = even.shape[1]
    rows = out.shape[3]
    low, high = bounds[0], bounds[1]
    centre = 0.5 * (high + low)
    scale = 1.0 / (0.5 * (high - low))
    row = lax.broadcasted_iota(jnp.int32, (height, width), 0)
    lane = lax.broadcasted_iota(jnp.int32, (height, width), 1)

    def beside(value):
        up = jnp.where(row == 0, 0.0, pltpu.roll(value, 1, 0))
        down = jnp.where(row == height - 1, 0.0, pltpu.roll(value, height - 1, 0))
        left = jnp.where(lane == 0, 0.0, pltpu.roll(value, 1, 1))
        right = jnp.where(lane == width - 1, 0.0, pltpu.roll(value, width - 1, 1))
        return (up + down) + (left + right)

    start = 0
    for source in (far_lo, lo, own, hi, far_hi):
        count = source.shape[0]

        def load(index, carry, source=source, start=start):
            label = source[index, local].astype(jnp.float32)
            root = jnp.where(label == 1.0, ROOTS[1], 0.0)
            root = jnp.where(label == 2.0, ROOTS[2], root)
            root = jnp.where(label == 3.0, ROOTS[3], root)
            strong[start + index] = root
            for mode in range(local):
                value = jnp.where(label > 0.0, source[index, mode].astype(jnp.float32), 0.0)
                even[start + index, mode] = value
                weak_even[start + index, mode] = root * value
            return carry

        lax.fori_loop(0, count, load, 0)
        start += count

    def weigh(plane, carry):
        root = strong[plane]
        degree[plane] = root * (strong[plane - 1] + strong[plane + 1] + beside(root))
        return carry

    lax.fori_loop(1, planes - 1, weigh, 0)

    cur, prev, weak, weak_next = even, odd, weak_even, weak_odd
    for step in range(DEGREE):
        factor = scale if step == 0 else 2.0 * scale

        def advance(plane, carry, cur=cur, prev=prev, weak=weak, weak_next=weak_next, factor=factor, step=step):
            root = strong[plane]
            here = (degree[plane] - centre) * factor
            there = root * factor
            for mode in range(local):
                around = weak[plane - 1, mode] + weak[plane + 1, mode] + beside(weak[plane, mode])
                value = here * cur[plane, mode] - there * around
                if step > 0:
                    value = value - prev[plane, mode]
                prev[plane, mode] = value
                weak_next[plane, mode] = root * value
            return carry

        lax.fori_loop(step + 1, planes - step - 1, advance, 0)
        cur, prev = prev, cur
        weak, weak_next = weak_next, weak

    def finish(index, carry):
        plane = REACH + index
        root, heavy = strong[plane], degree[plane]
        for mode in range(local):
            value = cur[plane, mode]
            around = weak[plane - 1, mode] + weak[plane + 1, mode] + beside(weak[plane, mode])
            image = heavy * value - root * around
            out[:, index, mode] = value.reshape(-1, rows, width).astype(out.dtype)
            out[:, index, local + mode] = image.reshape(-1, rows, width).astype(out.dtype)
        return carry

    lax.fori_loop(0, own.shape[0], finish, 0)


def filtered_and_applied(bounds, far_lo, lo, own, hi, far_hi, blocks):
    depth, fields, height, width = own.shape
    local = fields - 1
    planes = depth + 2 * REACH
    field = pltpu.VMEM((planes, local, height, width), jnp.float32)
    plane = pltpu.VMEM((planes, height, width), jnp.float32)
    vmem = pl.BlockSpec(memory_space=pltpu.VMEM)
    return pl.pallas_call(
        filter_kernel,
        out_shape=jax.ShapeDtypeStruct((blocks, depth, 2 * local, height // blocks, width), jnp.bfloat16),
        in_specs=[pl.BlockSpec(memory_space=pltpu.SMEM)] + [vmem] * 5,
        out_specs=vmem,
        scratch_shapes=[field, field, field, field, plane, plane],
        compiler_params=pltpu.CompilerParams(vmem_limit_bytes=40 * 1024 * 1024),
        name="chebyshev_filter",
    )(bounds, far_lo, lo, own, hi, far_hi)


def shifted(value, axis, step):
    size = lax.axis_size(axis)
    pairs = [(i, i + step) for i in range(size) if 0 <= i + step < size]
    return lax.ppermute(value, axis, pairs)


def exchanged(value, axis, mask):
    size = lax.axis_size(axis)
    return lax.ppermute(value, axis, [(i, i ^ mask) for i in range(size)])


def summed_over_z(value):
    for base in (1, 4):
        one = exchanged(value, "z", base)
        two = exchanged(value, "z", 2 * base)
        three = exchanged(value, "z", 3 * base)
        value = (value + one) + (two + three)
    return value


def total_over_all(partial):
    rows, columns = partial.shape
    peers = lax.axis_size(LAYER)
    chunk = 8
    padded = jnp.pad(partial, ((0, peers * chunk - rows), (0, 0))).reshape(peers, chunk, columns)
    terms = lax.all_to_all(padded, LAYER, 0, 0, tiled=True)
    mine = summed_over_z(jnp.sum(terms, axis=0))
    whole = lax.all_to_all(jnp.broadcast_to(mine, (peers, chunk, columns)), LAYER, 0, 0, tiled=True)
    return whole.reshape(peers * chunk, columns)[:rows]


def factor(gram, cross):
    lower = jnp.linalg.cholesky(gram)
    inverse = jax.scipy.linalg.solve_triangular(
        lower, jnp.eye(gram.shape[0], dtype=jnp.float32), lower=True
    )
    projected = jnp.dot(
        jnp.dot(inverse, cross, precision=lax.Precision.HIGHEST),
        inverse.T,
        precision=lax.Precision.HIGHEST,
    )
    return (projected, inverse.astype(jnp.bfloat16))


def per_device(initial_block, labels, filter_low, filter_high):
    share, _, height, width = initial_block.shape
    group, blocks = lax.axis_size(GROUP), lax.axis_size(MODE)
    local = share // group
    modes = share * blocks
    rows = height // blocks
    scale = math.sqrt(height * width * group * lax.axis_size("z"))

    fields = initial_block.reshape(group, local, height, width)
    tags = jnp.broadcast_to(labels.astype(jnp.bfloat16)[None], (group, 1, height, width))
    own = lax.all_to_all(jnp.concatenate([fields, tags], axis=1), GROUP, 0, 0, tiled=True)
    extra = REACH - group
    lo, hi = shifted(own, "z", 1), shifted(own, "z", -1)
    far_lo, far_hi = shifted(own[group - extra :], "z", 2), shifted(own[:extra], "z", -2)

    bounds = jnp.stack([filter_low, filter_high])
    pair = filtered_and_applied(bounds, far_lo, lo, own, hi, far_hi, blocks)
    pair = pair.reshape(blocks * group, 2 * local, rows, width)

    pair = lax.all_to_all(pair, LAYER, 0, 0, tiled=True)
    filtered = pair[:, :local].reshape(modes, rows * width)
    applied = pair[:, local:].reshape(modes, rows * width)
    both = jnp.concatenate([filtered, applied], axis=0)
    partial = jnp.einsum("mc,nc->mn", both, filtered, preferred_element_type=jnp.float32)
    total = total_over_all(partial)
    gram, cross = total[:modes], total[modes:].T
    projected, rotation = factor(gram, cross)
    turned = jnp.einsum("jm,mc->jc", rotation, filtered, preferred_element_type=jnp.float32)
    turned = (turned * scale).astype(jnp.bfloat16).reshape(blocks, share, rows, width)
    turned = lax.all_to_all(turned, MODE, 0, 0, tiled=True)
    modes_out = jnp.transpose(turned, (1, 0, 2, 3)).reshape(share, 1, height, width)
    return (modes_out, projected)


def solution(mesh):
    devices = mesh.devices
    slabs, modes = devices.shape
    fine = Mesh(devices.reshape(slabs // 4, 2, 2, 2, modes // 2), AXES)
    placed = (P(MODE, ("z",) + GROUP, None, None), P(("z",) + GROUP, None, None), P(), P())
    return jax.shard_map(
        per_device,
        mesh=fine,
        in_specs=placed,
        out_specs=(P(MODE, ("z",) + GROUP, None, None), P()),
        check_vma=False,
    )
```

```python
import functools
import math

import jax
import jax.numpy as jnp
from jax import lax
from jax.experimental import pallas as pl
from jax.experimental.pallas import tpu as pltpu
from jax.sharding import Mesh, PartitionSpec as P

DEGREE = 4
ROOTS = (0.0, 0.7745967, 1.0, 1.3416408)
REACH = DEGREE + 1
SUBLANES, LANES = 8, 128

AXES = ("z", "xl", "core", "xh", "y")
GROUP = ("xl", "core")
MODE = ("xh", "y")
LAYER = ("xh", "y", "xl", "core")


def filter_kernel(bounds, far_lo, lo, own, hi, far_hi, out, even, odd, weak_even, weak_odd, strong, degree):
    planes, height, width = strong.shape
    local = even.shape[1]
    rows = out.shape[3]
    low, high = bounds[0], bounds[1]
    centre = 0.5 * (high + low)
    scale = 1.0 / (0.5 * (high - low))
    row = lax.broadcasted_iota(jnp.int32, (height, width), 0)
    lane = lax.broadcasted_iota(jnp.int32, (height, width), 1)

    def beside(value):
        up = jnp.where(row == 0, 0.0, pltpu.roll(value, 1, 0))
        down = jnp.where(row == height - 1, 0.0, pltpu.roll(value, height - 1, 0))
        left = jnp.where(lane == 0, 0.0, pltpu.roll(value, 1, 1))
        right = jnp.where(lane == width - 1, 0.0, pltpu.roll(value, width - 1, 1))
        return (up + down) + (left + right)

    start = 0
    for source in (far_lo, lo, own, hi, far_hi):
        count = source.shape[0]

        def load(index, carry, source=source, start=start):
            label = source[index, local].astype(jnp.float32)
            root = jnp.where(label == 1.0, ROOTS[1], 0.0)
            root = jnp.where(label == 2.0, ROOTS[2], root)
            root = jnp.where(label == 3.0, ROOTS[3], root)
            strong[start + index] = root
            for mode in range(local):
                value = jnp.where(label > 0.0, source[index, mode].astype(jnp.float32), 0.0)
                even[start + index, mode] = value
                weak_even[start + index, mode] = root * value
            return carry

        lax.fori_loop(0, count, load, 0)
        start += count

    def weigh(plane, carry):
        root = strong[plane]
        degree[plane] = root * (strong[plane - 1] + strong[plane + 1] + beside(root))
        return carry

    lax.fori_loop(1, planes - 1, weigh, 0)

    cur, prev, weak, weak_next = even, odd, weak_even, weak_odd
    for step in range(DEGREE):
        factor = scale if step == 0 else 2.0 * scale

        def advance(plane, carry, cur=cur, prev=prev, weak=weak, weak_next=weak_next, factor=factor, step=step):
            root = strong[plane]
            here = (degree[plane] - centre) * factor
            there = root * factor
            for mode in range(local):
                around = weak[plane - 1, mode] + weak[plane + 1, mode] + beside(weak[plane, mode])
                value = here * cur[plane, mode] - there * around
                if step > 0:
                    value = value - prev[plane, mode]
                prev[plane, mode] = value
                weak_next[plane, mode] = root * value
            return carry

        lax.fori_loop(step + 1, planes - step - 1, advance, 0)
        cur, prev = prev, cur
        weak, weak_next = weak_next, weak

    def finish(index, carry):
        plane = REACH + index
        root, heavy = strong[plane], degree[plane]
        for mode in range(local):
            value = cur[plane, mode]
            around = weak[plane - 1, mode] + weak[plane + 1, mode] + beside(weak[plane, mode])
            image = heavy * value - root * around
            out[:, index, mode] = value.reshape(-1, rows, width).astype(out.dtype)
            out[:, index, local + mode] = image.reshape(-1, rows, width).astype(out.dtype)
        return carry

    lax.fori_loop(0, own.shape[0], finish, 0)


def filtered_and_applied(bounds, far_lo, lo, own, hi, far_hi, blocks):
    depth, fields, height, width = own.shape
    local = fields - 1
    planes = depth + 2 * REACH
    field = pltpu.VMEM((planes, local, height, width), jnp.float32)
    plane = pltpu.VMEM((planes, height, width), jnp.float32)
    vmem = pl.BlockSpec(memory_space=pltpu.VMEM)
    return pl.pallas_call(
        filter_kernel,
        out_shape=jax.ShapeDtypeStruct((blocks, depth, 2 * local, height // blocks, width), jnp.bfloat16),
        in_specs=[pl.BlockSpec(memory_space=pltpu.SMEM)] + [vmem] * 5,
        out_specs=vmem,
        scratch_shapes=[field, field, field, field, plane, plane],
        compiler_params=pltpu.CompilerParams(vmem_limit_bytes=40 * 1024 * 1024),
        name="chebyshev_filter",
    )(bounds, far_lo, lo, own, hi, far_hi)


def shifted(value, axis, step):
    size = lax.axis_size(axis)
    pairs = [(i, i + step) for i in range(size) if 0 <= i + step < size]
    return lax.ppermute(value, axis, pairs)


def summed_over_z(value):
    copies = jnp.broadcast_to(value, (lax.axis_size("z"),) + value.shape)
    return jnp.sum(lax.all_to_all(copies, "z", 0, 0, tiled=True), axis=0)


def total_over_all(partial):
    rows, columns = partial.shape
    peers = lax.axis_size(LAYER)
    chunk = 8
    padded = jnp.pad(partial, ((0, peers * chunk - rows), (0, 0))).reshape(peers, chunk, columns)
    terms = lax.all_to_all(padded, LAYER, 0, 0, tiled=True)
    mine = summed_over_z(jnp.sum(terms, axis=0))
    whole = lax.all_to_all(jnp.broadcast_to(mine, (peers, chunk, columns)), LAYER, 0, 0, tiled=True)
    return whole.reshape(peers * chunk, columns)[:rows]


def inverse_kernel(gram, out):
    groups = gram.shape[0] // SUBLANES
    tile = (SUBLANES, gram.shape[1])
    sub = lax.broadcasted_iota(jnp.int32, tile, 0)
    lane = lax.broadcasted_iota(jnp.int32, tile, 1)
    left = [gram[SUBLANES * g : SUBLANES * (g + 1), :] for g in range(groups)]
    right = [jnp.where(lane == sub + SUBLANES * g, 1.0, 0.0) for g in range(groups)]

    def row_of(value, t):
        return jnp.broadcast_to(value[t : t + 1, :], tile)

    for b in range(groups):
        first = SUBLANES * b
        columns = [
            [jnp.broadcast_to(left[g][:, first + t : first + t + 1], tile) for g in range(b, groups)]
            for t in range(SUBLANES)
        ]
        diagonal = jnp.ones(tile, jnp.float32)
        for t in range(SUBLANES):
            pivot = row_of(columns[t][0], t)
            diagonal = jnp.where(sub == t, pivot, diagonal)
            part = 1.0 / pivot
            row_left = row_of(left[b], t) * part
            row_right = row_of(right[b], t) * part
            rest = range(t + 1, SUBLANES)
            row_columns = [row_of(columns[s][0], t) * part for s in rest]
            for g in range(b, groups):
                weight = columns[t][g - b]
                if g == b:
                    weight = jnp.where(sub > t, weight, 0.0)
                left[g] = left[g] - weight * row_left
                right[g] = right[g] - weight * row_right
                for s, row_column in zip(rest, row_columns):
                    columns[s][g - b] = columns[s][g - b] - weight * row_column
        out[first : first + SUBLANES, :] = right[b] * lax.rsqrt(diagonal)


def inverse_factor(gram):
    size = gram.shape[0]
    padded = jnp.pad(gram, ((0, 0), (0, LANES - size)))
    vmem = pl.BlockSpec(memory_space=pltpu.VMEM)
    inverse = pl.pallas_call(
        inverse_kernel,
        out_shape=jax.ShapeDtypeStruct(padded.shape, jnp.float32),
        in_specs=[vmem],
        out_specs=vmem,
        name="inverse_factor",
    )(padded)
    return inverse[:, :size]


def projection(inverse, cross):
    return jnp.dot(
        jnp.dot(inverse, cross, precision=lax.Precision.HIGHEST),
        inverse.T,
        precision=lax.Precision.HIGHEST,
    )


def per_device(initial_block, labels, filter_low, filter_high):
    share, _, height, width = initial_block.shape
    group, blocks = lax.axis_size(GROUP), lax.axis_size(MODE)
    local = share // group
    modes = share * blocks
    rows = height // blocks
    scale = math.sqrt(height * width * group * lax.axis_size("z"))

    fields = initial_block.reshape(group, local, height, width)
    tags = jnp.broadcast_to(labels.astype(jnp.bfloat16)[None], (group, 1, height, width))
    own = lax.all_to_all(jnp.concatenate([fields, tags], axis=1), GROUP, 0, 0, tiled=True)
    extra = REACH - group
    lo, hi = shifted(own, "z", 1), shifted(own, "z", -1)
    far_lo, far_hi = shifted(own[group - extra :], "z", 2), shifted(own[:extra], "z", -2)

    bounds = jnp.stack([filter_low, filter_high])
    pair = filtered_and_applied(bounds, far_lo, lo, own, hi, far_hi, blocks)
    pair = pair.reshape(blocks * group, 2 * local, rows, width)

    pair = lax.all_to_all(pair, LAYER, 0, 0, tiled=True)
    filtered = pair[:, :local].reshape(modes, rows * width)
    applied = pair[:, local:].reshape(modes, rows * width)
    both = jnp.concatenate([filtered, applied], axis=0)
    partial = jnp.einsum("mc,nc->mn", both, filtered, preferred_element_type=jnp.float32)
    total = total_over_all(partial)
    gram, cross = total[:modes], total[modes:].T
    inverse = inverse_factor(gram)
    projected = projection(inverse, cross)
    turned = jnp.einsum("jm,mc->jc", inverse.astype(jnp.bfloat16), filtered, preferred_element_type=jnp.float32)
    turned = (turned * scale).astype(jnp.bfloat16).reshape(blocks, share, rows, width)
    turned = lax.all_to_all(turned, MODE, 0, 0, tiled=True)
    modes_out = jnp.transpose(turned, (1, 0, 2, 3)).reshape(share, 1, height, width)
    return (modes_out, projected)


def solution(mesh):
    devices = mesh.devices
    slabs, modes = devices.shape
    fine = Mesh(devices.reshape(slabs // 4, 2, 2, 2, modes // 2), AXES)
    placed = (P(MODE, ("z",) + GROUP, None, None), P(("z",) + GROUP, None, None), P(), P())
    return jax.shard_map(
        per_device,
        mesh=fine,
        in_specs=placed,
        out_specs=(P(MODE, ("z",) + GROUP, None, None), P()),
        check_vma=False,
    )
```

```python
import functools
import math

import jax
import jax.numpy as jnp
from jax import lax
from jax.experimental import pallas as pl
from jax.experimental.pallas import tpu as pltpu
from jax.sharding import Mesh, PartitionSpec as P

DEGREE = 4
ROOTS = (0.0, 0.7745967, 1.0, 1.3416408)
REACH = DEGREE + 1
SUBLANES = 8
UNROLL = 4

AXES = ("z", "xl", "core", "xh", "y")
GROUP = ("xl", "core")
MODE = ("xh", "y")
LAYER = ("xh", "y", "xl", "core")


def filter_kernel(bounds, far_lo, lo, own, hi, far_hi, out, even, odd, weak_even, weak_odd, strong, degree):
  planes, height, width = degree.shape
  local = even.shape[1]
  rows = out.shape[3]
  low, high = bounds[0], bounds[1]
  centre = 0.5 * (high + low)
  scale = 1.0 / (0.5 * (high - low))
  inner = pl.ds(SUBLANES, height)
  lane = lax.broadcasted_iota(jnp.int32, (height, width), 1)

  def beside(ref, *index):
      value = ref[(*index, inner)]
      up = ref[(*index, pl.ds(SUBLANES - 1, height))]
      down = ref[(*index, pl.ds(SUBLANES + 1, height))]
      left = jnp.where(lane == 0, 0.0, pltpu.roll(value, 1, 1))
      right = jnp.where(lane == width - 1, 0.0, pltpu.roll(value, width - 1, 1))
      return value, (up + down) + (left + right)

  edge = jnp.zeros((SUBLANES, width), jnp.float32)

  def clear(plane, carry):
      for first in (0, SUBLANES + height):
          strong[plane, pl.ds(first, SUBLANES)] = edge
          for mode in range(local):
              weak_even[plane, mode, pl.ds(first, SUBLANES)] = edge
              weak_odd[plane, mode, pl.ds(first, SUBLANES)] = edge
      return carry

  lax.fori_loop(0, planes, clear, 0)

  start = 0
  for source in (far_lo, lo, own, hi, far_hi):
      count = source.shape[0]

      def load(index, carry, source=source, start=start):
          label = source[index, local].astype(jnp.float32)
          root = jnp.where(label == 1.0, ROOTS[1], 0.0)
          root = jnp.where(label == 2.0, ROOTS[2], root)
          root = jnp.where(label == 3.0, ROOTS[3], root)
          strong[start + index, inner] = root
          for mode in range(local):
              value = jnp.where(label > 0.0, source[index, mode].astype(jnp.float32), 0.0)
              even[start + index, mode] = value
              weak_even[start + index, mode, inner] = root * value
          return carry

      lax.fori_loop(0, count, load, 0, unroll=min(count, UNROLL))
      start += count

  def weigh(plane, carry):
      root, around = beside(strong, plane)
      degree[plane] = root * (strong[plane - 1, inner] + strong[plane + 1, inner] + around)
      return carry

  lax.fori_loop(1, planes - 1, weigh, 0, unroll=UNROLL)

  cur, prev, weak, weak_next = even, odd, weak_even, weak_odd
  for step in range(DEGREE):
      factor = scale if step == 0 else 2.0 * scale

      def advance(plane, carry, cur=cur, prev=prev, weak=weak, weak_next=weak_next, factor=factor, step=step):
          root = strong[plane, inner]
          here = (degree[plane] - centre) * factor
          there = root * factor
          for mode in range(local):
              _, around = beside(weak, plane, mode)
              around = around + (weak[plane - 1, mode, inner] + weak[plane + 1, mode, inner])
              value = here * cur[plane, mode] - there * around
              if step > 0:
                  value = value - prev[plane, mode]
              prev[plane, mode] = value
              weak_next[plane, mode, inner] = root * value
          return carry

      lax.fori_loop(step + 1, planes - step - 1, advance, 0, unroll=UNROLL)
      cur, prev = prev, cur
      weak, weak_next = weak_next, weak

  def finish(index, carry):
      plane = REACH + index
      root, heavy = strong[plane, inner], degree[plane]
      for mode in range(local):
          value = cur[plane, mode]
          _, around = beside(weak, plane, mode)
          around = around + (weak[plane - 1, mode, inner] + weak[plane + 1, mode, inner])
          image = heavy * value - root * around
          out[:, index, mode] = value.reshape(-1, rows, width).astype(out.dtype)
          out[:, index, local + mode] = image.reshape(-1, rows, width).astype(out.dtype)
      return carry

  lax.fori_loop(0, own.shape[0], finish, 0, unroll=2)

def filtered_and_applied(bounds, far_lo, lo, own, hi, far_hi, blocks):
    depth, fields, height, width = own.shape
    local = fields - 1
    planes = depth + 2 * REACH
    field = pltpu.VMEM((planes, local, height, width), jnp.float32)
    rimmed = pltpu.VMEM((planes, local, height + 2 * SUBLANES, width), jnp.float32)
    root = pltpu.VMEM((planes, height + 2 * SUBLANES, width), jnp.float32)
    degree = pltpu.VMEM((planes, height, width), jnp.float32)
    vmem = pl.BlockSpec(memory_space=pltpu.VMEM)
    return pl.pallas_call(
        filter_kernel,
        out_shape=jax.ShapeDtypeStruct((blocks, depth, 2 * local, height // blocks, width), jnp.bfloat16),
        in_specs=[pl.BlockSpec(memory_space=pltpu.SMEM)] + [vmem] * 5,
        out_specs=vmem,
        scratch_shapes=[field, field, rimmed, rimmed, root, degree],
        compiler_params=pltpu.CompilerParams(vmem_limit_bytes=40 * 1024 * 1024),
        name="chebyshev_filter",
    )(bounds, far_lo, lo, own, hi, far_hi)


def pack_kernel(block, labels, out):
    group, fields = out.shape[:2]
    local = fields - 1
    tags = labels[0].astype(jnp.float32).astype(out.dtype)
    for peer in range(group):
        for mode in range(local):
            out[peer, mode] = block[peer * local + mode, 0]
        out[peer, local] = tags


def packed(block, labels, group):
    share, _, height, width = block.shape
    vmem = pl.BlockSpec(memory_space=pltpu.VMEM)
    return pl.pallas_call(
        pack_kernel,
        out_shape=jax.ShapeDtypeStruct((group, share // group + 1, height, width), block.dtype),
        in_specs=[vmem, vmem],
        out_specs=vmem,
        name="pack",
    )(block, labels)


def shifted(value, axis, step):
    size = lax.axis_size(axis)
    pairs = [(i, i + step) for i in range(size) if 0 <= i + step < size]
    return lax.ppermute(value, axis, pairs)


def summed_over_z(value):
    copies = jnp.broadcast_to(value, (lax.axis_size("z"),) + value.shape)
    return jnp.sum(lax.all_to_all(copies, "z", 0, 0, tiled=True), axis=0)


def total_over_all(partial):
    rows, columns = partial.shape
    peers = lax.axis_size(LAYER)
    chunk = 8
    padded = jnp.pad(partial, ((0, peers * chunk - rows), (0, 0))).reshape(peers, chunk, columns)
    terms = lax.all_to_all(padded, LAYER, 0, 0, tiled=True)
    mine = summed_over_z(jnp.sum(terms, axis=0))
    whole = lax.all_to_all(jnp.broadcast_to(mine, (peers, chunk, columns)), LAYER, 0, 0, tiled=True)
    return whole


def turn_kernel(scale, whole, filtered, inverse, turned, staged):
    size = inverse.shape[0]
    rows = turned.shape[2]
    groups = size // SUBLANES
    tile = (SUBLANES, size)
    sub = lax.broadcasted_iota(jnp.int32, tile, 0)
    lane = lax.broadcasted_iota(jnp.int32, tile, 1)
    left = [whole[g] for g in range(groups)]
    right = [jnp.where(lane == sub + SUBLANES * g, 1.0, 0.0) for g in range(groups)]

    def row_of(value, t):
        return jnp.broadcast_to(value[t : t + 1, :], tile)

    for b in range(groups):
        first = SUBLANES * b
        columns = [
            [jnp.broadcast_to(left[g][:, first + t : first + t + 1], tile) for g in range(b, groups)]
            for t in range(SUBLANES)
        ]
        diagonal = jnp.ones(tile, jnp.float32)
        for t in range(SUBLANES):
            pivot = row_of(columns[t][0], t)
            diagonal = jnp.where(sub == t, pivot, diagonal)
            part = 1.0 / pivot
            row_left = row_of(left[b], t) * part
            row_right = row_of(right[b], t) * part
            rest = range(t + 1, SUBLANES)
            row_columns = [row_of(columns[s][0], t) * part for s in rest]
            for g in range(b, groups):
                weight = columns[t][g - b]
                if g == b:
                    weight = jnp.where(sub > t, weight, 0.0)
                left[g] = left[g] - weight * row_left
                right[g] = right[g] - weight * row_right
                for s, row_column in zip(rest, row_columns):
                    columns[s][g - b] = columns[s][g - b] - weight * row_column
        inverse[first : first + SUBLANES, :] = right[b] * lax.rsqrt(diagonal)

    rotation = inverse[...].astype(jnp.bfloat16)
    product = jnp.dot(rotation, filtered[...], preferred_element_type=jnp.float32) * scale
    width = turned.shape[3]
    for row in range(rows):
        staged[pl.ds(row, size, stride=rows), :] = product[:, row * width : (row + 1) * width]
    turned[...] = staged[...].reshape(turned.shape).astype(turned.dtype)


def inverse_and_turned(whole, filtered, scale, peers, rows):
    size = whole.shape[2]
    width = filtered.shape[1] // rows
    vmem = pl.BlockSpec(memory_space=pltpu.VMEM)
    return pl.pallas_call(
        functools.partial(turn_kernel, scale),
        out_shape=(
            jax.ShapeDtypeStruct((size, size), jnp.float32),
            jax.ShapeDtypeStruct((peers, size // peers, rows, width), jnp.bfloat16),
        ),
        in_specs=[vmem, vmem],
        out_specs=(vmem, vmem),
        scratch_shapes=[pltpu.VMEM((size * rows, width), jnp.float32)],
        name="inverse_and_turned",
    )(whole, filtered)


def projection(inverse, cross):
    return jnp.dot(
        jnp.dot(inverse, cross, precision=lax.Precision.HIGHEST),
        inverse.T,
        precision=lax.Precision.HIGHEST,
    )


def per_device(initial_block, labels, filter_low, filter_high):
    share, _, height, width = initial_block.shape
    group, blocks = lax.axis_size(GROUP), lax.axis_size(MODE)
    local = share // group
    modes = share * blocks
    rows = height // blocks
    scale = math.sqrt(height * width * group * lax.axis_size("z"))

    own = lax.all_to_all(packed(initial_block, labels, group), GROUP, 0, 0, tiled=True)
    extra = REACH - group
    lo, hi = shifted(own, "z", 1), shifted(own, "z", -1)
    far_lo, far_hi = shifted(own[group - extra :], "z", 2), shifted(own[:extra], "z", -2)

    bounds = jnp.stack([filter_low, filter_high])
    pair = filtered_and_applied(bounds, far_lo, lo, own, hi, far_hi, blocks)
    pair = pair.reshape(blocks * group, 2 * local, rows, width)

    pair = lax.all_to_all(pair, LAYER, 0, 0, tiled=True)
    filtered = pair[:, :local].reshape(modes, rows * width)
    applied = pair[:, local:].reshape(modes, rows * width)
    both = jnp.concatenate([filtered, applied], axis=0)
    partial = jnp.einsum("mc,nc->mn", both, filtered, preferred_element_type=jnp.float32)
    total = total_over_all(partial)
    inverse, turned = inverse_and_turned(total, filtered, scale, blocks, rows)
    cross = total.reshape(-1, modes)[modes : 2 * modes].T
    projected = projection(inverse, cross)
    turned = lax.all_to_all(turned, MODE, 0, 0, tiled=True)
    modes_out = jnp.transpose(turned, (1, 0, 2, 3)).reshape(share, 1, height, width)
    return (modes_out, projected)


def solution(mesh):
    devices = mesh.devices
    slabs, modes = devices.shape
    fine = Mesh(devices.reshape(slabs // 4, 2, 2, 2, modes // 2), AXES)
    placed = (P(MODE, ("z",) + GROUP, None, None), P(("z",) + GROUP, None, None), P(), P())
    return jax.shard_map(
        per_device,
        mesh=fine,
        in_specs=placed,
        out_specs=(P(MODE, ("z",) + GROUP, None, None), P()),
        check_vma=False,
    )
```

```python
import functools
import math

import jax
import jax.numpy as jnp
from jax import lax
from jax.experimental import pallas as pl
from jax.experimental.pallas import tpu as pltpu
from jax.sharding import Mesh, PartitionSpec as P

DEGREE = 4
ROOTS = (0.0, 0.7745967, 1.0, 1.3416408)
REACH = DEGREE + 1
SUBLANES = 8
UNROLL = 4

AXES = ("z", "xl", "core", "xh", "y")
GROUP = ("xl", "core")
MODE = ("xh", "y")
LAYER = ("xh", "y", "xl", "core")


def filter_kernel(bounds, odd_z, own, pair, other, far_pair, far_other, out, even, odd, weak_even, weak_odd, strong, degree):
    planes, height, width = degree.shape
    local = even.shape[1]
    rows = out.shape[3]
    low, high = bounds[0], bounds[1]
    centre = 0.5 * (high + low)
    scale = 1.0 / (0.5 * (high - low))
    inner = pl.ds(SUBLANES, height)
    lane = lax.broadcasted_iota(jnp.int32, (height, width), 1)

    def beside(ref, *index):
        value = ref[(*index, inner)]
        up = ref[(*index, pl.ds(SUBLANES - 1, height))]
        down = ref[(*index, pl.ds(SUBLANES + 1, height))]
        left = jnp.where(lane == 0, 0.0, pltpu.roll(value, 1, 1))
        right = jnp.where(lane == width - 1, 0.0, pltpu.roll(value, width - 1, 1))
        return value, (up + down) + (left + right)

    edge = jnp.zeros((SUBLANES, width), jnp.float32)

    def clear(plane, carry):
        for first in (0, SUBLANES + height):
            strong[plane, pl.ds(first, SUBLANES)] = edge
            for mode in range(local):
                weak_even[plane, mode, pl.ds(first, SUBLANES)] = edge
                weak_odd[plane, mode, pl.ds(first, SUBLANES)] = edge
        return carry

    lax.fori_loop(0, planes, clear, 0)

    depth, extra = own.shape[0], far_pair.shape[0]
    side = odd_z[0]
    below, above, farthest = extra, REACH + depth, planes - extra
    for source, start in (
        (own, REACH),
        (pair, jnp.where(side == 0, above, below)),
        (other, jnp.where(side == 0, below, above)),
        (far_pair, jnp.where(side == 0, farthest, 0)),
        (far_other, jnp.where(side == 0, 0, farthest)),
    ):
        count = source.shape[0]

        def load(index, carry, source=source, start=start):
            label = source[index, local].astype(jnp.float32)
            root = jnp.where(label == 1.0, ROOTS[1], 0.0)
            root = jnp.where(label == 2.0, ROOTS[2], root)
            root = jnp.where(label == 3.0, ROOTS[3], root)
            strong[start + index, inner] = root
            for mode in range(local):
                value = jnp.where(label > 0.0, source[index, mode].astype(jnp.float32), 0.0)
                even[start + index, mode] = value
                weak_even[start + index, mode, inner] = root * value
            return carry

        lax.fori_loop(0, count, load, 0, unroll=min(count, UNROLL))

    def weigh(plane, carry):
        root, around = beside(strong, plane)
        degree[plane] = root * (strong[plane - 1, inner] + strong[plane + 1, inner] + around)
        return carry

    lax.fori_loop(1, planes - 1, weigh, 0, unroll=UNROLL)

    cur, prev, weak, weak_next = even, odd, weak_even, weak_odd
    for step in range(DEGREE):
        factor = scale if step == 0 else 2.0 * scale

        def advance(plane, carry, cur=cur, prev=prev, weak=weak, weak_next=weak_next, factor=factor, step=step):
            root = strong[plane, inner]
            here = (degree[plane] - centre) * factor
            there = root * factor
            for mode in range(local):
                _, around = beside(weak, plane, mode)
                around = around + (weak[plane - 1, mode, inner] + weak[plane + 1, mode, inner])
                value = here * cur[plane, mode] - there * around
                if step > 0:
                    value = value - prev[plane, mode]
                prev[plane, mode] = value
                weak_next[plane, mode, inner] = root * value
            return carry

        lax.fori_loop(step + 1, planes - step - 1, advance, 0, unroll=UNROLL)
        cur, prev = prev, cur
        weak, weak_next = weak_next, weak

    def finish(index, carry):
        plane = REACH + index
        root, heavy = strong[plane, inner], degree[plane]
        for mode in range(local):
            value = cur[plane, mode]
            _, around = beside(weak, plane, mode)
            around = around + (weak[plane - 1, mode, inner] + weak[plane + 1, mode, inner])
            image = heavy * value - root * around
            out[:, index, mode] = value.reshape(-1, rows, width).astype(out.dtype)
            out[:, index, local + mode] = image.reshape(-1, rows, width).astype(out.dtype)
        return carry

    lax.fori_loop(0, own.shape[0], finish, 0, unroll=2)

def filtered_and_applied(bounds, odd_z, own, pair, other, far_pair, far_other, blocks):
    depth, fields, height, width = own.shape
    local = fields - 1
    planes = depth + 2 * REACH
    field = pltpu.VMEM((planes, local, height, width), jnp.float32)
    rimmed = pltpu.VMEM((planes, local, height + 2 * SUBLANES, width), jnp.float32)
    root = pltpu.VMEM((planes, height + 2 * SUBLANES, width), jnp.float32)
    degree = pltpu.VMEM((planes, height, width), jnp.float32)
    vmem = pl.BlockSpec(memory_space=pltpu.VMEM)
    return pl.pallas_call(
        filter_kernel,
        out_shape=jax.ShapeDtypeStruct((blocks, depth, 2 * local, height // blocks, width), jnp.bfloat16),
        in_specs=[pl.BlockSpec(memory_space=pltpu.SMEM)] * 2 + [vmem] * 5,
        out_specs=vmem,
        scratch_shapes=[field, field, rimmed, rimmed, root, degree],
        compiler_params=pltpu.CompilerParams(vmem_limit_bytes=40 * 1024 * 1024),
        name="chebyshev_filter",
    )(bounds, odd_z, own, pair, other, far_pair, far_other)


def pack_kernel(block, labels, out):
    group, fields = out.shape[:2]
    local = fields - 1
    tags = labels[0].astype(jnp.float32).astype(out.dtype)
    for peer in range(group):
        for mode in range(local):
            out[peer, mode] = block[peer * local + mode, 0]
        out[peer, local] = tags


def packed(block, labels, group):
    share, _, height, width = block.shape
    vmem = pl.BlockSpec(memory_space=pltpu.VMEM)
    return pl.pallas_call(
        pack_kernel,
        out_shape=jax.ShapeDtypeStruct((group, share // group + 1, height, width), block.dtype),
        in_specs=[vmem, vmem],
        out_specs=vmem,
        name="pack",
    )(block, labels)


def traded(value, step):
    size = lax.axis_size("z")
    pairs = [(z, z + step(z)) for z in range(size) if 0 <= z + step(z) < size]
    return lax.ppermute(value, "z", pairs)


def summed_over_z(value):
    copies = jnp.broadcast_to(value, (lax.axis_size("z"),) + value.shape)
    return jnp.sum(lax.all_to_all(copies, "z", 0, 0, tiled=True), axis=0)


def total_over_all(partial):
    rows, columns = partial.shape
    peers = lax.axis_size(LAYER)
    chunk = 8
    padded = jnp.pad(partial, ((0, peers * chunk - rows), (0, 0))).reshape(peers, chunk, columns)
    terms = lax.all_to_all(padded, LAYER, 0, 0, tiled=True)
    mine = summed_over_z(jnp.sum(terms, axis=0))
    whole = lax.all_to_all(jnp.broadcast_to(mine, (peers, chunk, columns)), LAYER, 0, 0, tiled=True)
    return whole


def turn_kernel(scale, whole, filtered, inverse, turned, staged):
    size = inverse.shape[0]
    rows = turned.shape[2]
    groups = size // SUBLANES
    tile = (SUBLANES, size)
    sub = lax.broadcasted_iota(jnp.int32, tile, 0)
    lane = lax.broadcasted_iota(jnp.int32, tile, 1)
    left = [whole[g] for g in range(groups)]
    right = [jnp.where(lane == sub + SUBLANES * g, 1.0, 0.0) for g in range(groups)]

    def row_of(value, t):
        return jnp.broadcast_to(value[t : t + 1, :], tile)

    for b in range(groups):
        first = SUBLANES * b
        columns = [
            [jnp.broadcast_to(left[g][:, first + t : first + t + 1], tile) for g in range(b, groups)]
            for t in range(SUBLANES)
        ]
        diagonal = jnp.ones(tile, jnp.float32)
        for t in range(SUBLANES):
            pivot = row_of(columns[t][0], t)
            diagonal = jnp.where(sub == t, pivot, diagonal)
            part = 1.0 / pivot
            row_left = row_of(left[b], t) * part
            row_right = row_of(right[b], t) * part
            rest = range(t + 1, SUBLANES)
            row_columns = [row_of(columns[s][0], t) * part for s in rest]
            for g in range(b, groups):
                weight = columns[t][g - b]
                if g == b:
                    weight = jnp.where(sub > t, weight, 0.0)
                left[g] = left[g] - weight * row_left
                right[g] = right[g] - weight * row_right
                for s, row_column in zip(rest, row_columns):
                    columns[s][g - b] = columns[s][g - b] - weight * row_column
        inverse[first : first + SUBLANES, :] = right[b] * lax.rsqrt(diagonal)

    rotation = inverse[...].astype(jnp.bfloat16)
    product = jnp.dot(rotation, filtered[...], preferred_element_type=jnp.float32) * scale
    width = turned.shape[3]
    for row in range(rows):
        staged[pl.ds(row, size, stride=rows), :] = product[:, row * width : (row + 1) * width]
    turned[...] = staged[...].reshape(turned.shape).astype(turned.dtype)


def inverse_and_turned(whole, filtered, scale, peers, rows):
    size = whole.shape[2]
    width = filtered.shape[1] // rows
    vmem = pl.BlockSpec(memory_space=pltpu.VMEM)
    return pl.pallas_call(
        functools.partial(turn_kernel, scale),
        out_shape=(
            jax.ShapeDtypeStruct((size, size), jnp.float32),
            jax.ShapeDtypeStruct((peers, size // peers, rows, width), jnp.bfloat16),
        ),
        in_specs=[vmem, vmem],
        out_specs=(vmem, vmem),
        scratch_shapes=[pltpu.VMEM((size * rows, width), jnp.float32)],
        name="inverse_and_turned",
    )(whole, filtered)


def projection(inverse, cross):
    return jnp.dot(
        jnp.dot(inverse, cross, precision=lax.Precision.HIGHEST),
        inverse.T,
        precision=lax.Precision.HIGHEST,
    )


def per_device(initial_block, labels, filter_low, filter_high):
    share, _, height, width = initial_block.shape
    group, blocks = lax.axis_size(GROUP), lax.axis_size(MODE)
    local = share // group
    modes = share * blocks
    rows = height // blocks
    scale = math.sqrt(height * width * group * lax.axis_size("z"))

    own = lax.all_to_all(packed(initial_block, labels, group), GROUP, 0, 0, tiled=True)
    extra = REACH - group
    odd_z = lax.axis_index("z") % 2
    pair = traded(own, lambda z: 1 - 2 * (z % 2))
    other = traded(own, lambda z: 2 * (z % 2) - 1)
    far_pair = traded(lax.dynamic_slice_in_dim(own, odd_z * (group - extra), extra), lambda z: 4 * (z % 2) - 2)
    far_other = traded(lax.dynamic_slice_in_dim(own, (1 - odd_z) * (group - extra), extra), lambda z: 2 - 4 * (z % 2))

    bounds = jnp.stack([filter_low, filter_high])
    side = jnp.reshape(odd_z, (1,)).astype(jnp.int32)
    both = filtered_and_applied(bounds, side, own, pair, other, far_pair, far_other, blocks)
    both = both.reshape(blocks * group, 2 * local, rows, width)

    both = lax.all_to_all(both, LAYER, 0, 0, tiled=True)
    filtered = both[:, :local].reshape(modes, rows * width)
    applied = both[:, local:].reshape(modes, rows * width)
    both = jnp.concatenate([filtered, applied], axis=0)
    partial = jnp.einsum("mc,nc->mn", both, filtered, preferred_element_type=jnp.float32)
    total = total_over_all(partial)
    inverse, turned = inverse_and_turned(total, filtered, scale, blocks, rows)
    cross = total.reshape(-1, modes)[modes : 2 * modes].T
    projected = projection(inverse, cross)
    turned = lax.all_to_all(turned, MODE, 0, 0, tiled=True)
    modes_out = jnp.transpose(turned, (1, 0, 2, 3)).reshape(share, 1, height, width)
    return (modes_out, projected)


def solution(mesh):
    devices = mesh.devices
    slabs, modes = devices.shape
    fine = Mesh(devices.reshape(slabs // 4, 2, 2, 2, modes // 2), AXES)
    placed = (P(MODE, ("z",) + GROUP, None, None), P(("z",) + GROUP, None, None), P(), P())
    return jax.shard_map(
        per_device,
        mesh=fine,
        in_specs=placed,
        out_specs=(P(MODE, ("z",) + GROUP, None, None), P()),
        check_vma=False,
    )
```

```python
import functools
import math

import jax
import jax.numpy as jnp
from jax import lax
from jax.experimental import pallas as pl
from jax.experimental.pallas import tpu as pltpu
from jax.sharding import Mesh, PartitionSpec as P

DEGREE = 4
ROOTS = (0.0, 0.7745967, 1.0, 1.3416408)
REACH = DEGREE + 1
SUBLANES, LANES = 8, 128
UNROLL = 4

AXES = ("z", "xl", "core", "xh", "y")
GROUP = ("xl", "core")
MODE = ("xh", "y")
LAYER = ("xh", "y", "xl", "core")


def filter_kernel(bounds, far_lo, lo, own, hi, far_hi, out, even, odd, weak_even, weak_odd, strong, degree):
    planes, height, width = degree.shape
    local = even.shape[1]
    rows = out.shape[3]
    low, high = bounds[0], bounds[1]
    centre = 0.5 * (high + low)
    scale = 1.0 / (0.5 * (high - low))
    inner = pl.ds(SUBLANES, height)
    lane = lax.broadcasted_iota(jnp.int32, (height, width), 1)

    def beside(ref, *index):
        value = ref[(*index, inner)]
        up = ref[(*index, pl.ds(SUBLANES - 1, height))]
        down = ref[(*index, pl.ds(SUBLANES + 1, height))]
        left = jnp.where(lane == 0, 0.0, pltpu.roll(value, 1, 1))
        right = jnp.where(lane == width - 1, 0.0, pltpu.roll(value, width - 1, 1))
        return value, (up + down) + (left + right)

    edge = jnp.zeros((SUBLANES, width), jnp.float32)

    def clear(plane, carry):
        for first in (0, SUBLANES + height):
            strong[plane, pl.ds(first, SUBLANES)] = edge
            for mode in range(local):
                weak_even[plane, mode, pl.ds(first, SUBLANES)] = edge
                weak_odd[plane, mode, pl.ds(first, SUBLANES)] = edge
        return carry

    lax.fori_loop(0, planes, clear, 0)

    start = 0
    for source in (far_lo, lo, own, hi, far_hi):
        count = source.shape[0]

        def load(index, carry, source=source, start=start):
            label = source[index, local].astype(jnp.float32)
            root = jnp.where(label == 1.0, ROOTS[1], 0.0)
            root = jnp.where(label == 2.0, ROOTS[2], root)
            root = jnp.where(label == 3.0, ROOTS[3], root)
            strong[start + index, inner] = root
            for mode in range(local):
                value = jnp.where(label > 0.0, source[index, mode].astype(jnp.float32), 0.0)
                even[start + index, mode] = value
                weak_even[start + index, mode, inner] = root * value
            return carry

        lax.fori_loop(0, count, load, 0, unroll=min(count, UNROLL))
        start += count

    def weigh(plane, carry):
        root, around = beside(strong, plane)
        degree[plane] = root * (strong[plane - 1, inner] + strong[plane + 1, inner] + around)
        return carry

    lax.fori_loop(1, planes - 1, weigh, 0, unroll=UNROLL)

    cur, prev, weak, weak_next = even, odd, weak_even, weak_odd
    for step in range(DEGREE):
        factor = scale if step == 0 else 2.0 * scale

        def advance(plane, carry, cur=cur, prev=prev, weak=weak, weak_next=weak_next, factor=factor, step=step):
            root = strong[plane, inner]
            here = (degree[plane] - centre) * factor
            there = root * factor
            for mode in range(local):
                _, around = beside(weak, plane, mode)
                around = around + (weak[plane - 1, mode, inner] + weak[plane + 1, mode, inner])
                value = here * cur[plane, mode] - there * around
                if step > 0:
                    value = value - prev[plane, mode]
                prev[plane, mode] = value
                weak_next[plane, mode, inner] = root * value
            return carry

        lax.fori_loop(step + 1, planes - step - 1, advance, 0, unroll=UNROLL)
        cur, prev = prev, cur
        weak, weak_next = weak_next, weak

    def finish(index, carry):
        plane = REACH + index
        root, heavy = strong[plane, inner], degree[plane]
        for mode in range(local):
            value = cur[plane, mode]
            _, around = beside(weak, plane, mode)
            around = around + (weak[plane - 1, mode, inner] + weak[plane + 1, mode, inner])
            image = heavy * value - root * around
            out[:, index, mode] = value.reshape(-1, rows, width).astype(out.dtype)
            out[:, index, local + mode] = image.reshape(-1, rows, width).astype(out.dtype)
        return carry

    lax.fori_loop(0, own.shape[0], finish, 0, unroll=2)

def filtered_and_applied(bounds, far_lo, lo, own, hi, far_hi, blocks):
    depth, fields, height, width = own.shape
    local = fields - 1
    planes = depth + 2 * REACH
    field = pltpu.VMEM((planes, local, height, width), jnp.float32)
    rimmed = pltpu.VMEM((planes, local, height + 2 * SUBLANES, width), jnp.float32)
    root = pltpu.VMEM((planes, height + 2 * SUBLANES, width), jnp.float32)
    degree = pltpu.VMEM((planes, height, width), jnp.float32)
    vmem = pl.BlockSpec(memory_space=pltpu.VMEM)
    return pl.pallas_call(
        filter_kernel,
        out_shape=jax.ShapeDtypeStruct((blocks, depth, 2 * local, height // blocks, width), jnp.bfloat16),
        in_specs=[pl.BlockSpec(memory_space=pltpu.SMEM)] + [vmem] * 5,
        out_specs=vmem,
        scratch_shapes=[field, field, rimmed, rimmed, root, degree],
        compiler_params=pltpu.CompilerParams(vmem_limit_bytes=40 * 1024 * 1024),
        name="chebyshev_filter",
    )(bounds, far_lo, lo, own, hi, far_hi)


def pack_kernel(block, labels, out):
    group, fields = out.shape[:2]
    local = fields - 1
    tags = labels[0].astype(jnp.float32).astype(out.dtype)
    for peer in range(group):
        for mode in range(local):
            out[peer, mode] = block[peer * local + mode, 0]
        out[peer, local] = tags


def packed(block, labels, group):
    share, _, height, width = block.shape
    vmem = pl.BlockSpec(memory_space=pltpu.VMEM)
    return pl.pallas_call(
        pack_kernel,
        out_shape=jax.ShapeDtypeStruct((group, share // group + 1, height, width), block.dtype),
        in_specs=[vmem, vmem],
        out_specs=vmem,
        name="pack",
    )(block, labels)


def shifted(value, axis, step):
    size = lax.axis_size(axis)
    pairs = [(i, i + step) for i in range(size) if 0 <= i + step < size]
    return lax.ppermute(value, axis, pairs)


def summed_over_z(value):
    copies = jnp.broadcast_to(value, (lax.axis_size("z"),) + value.shape)
    return jnp.sum(lax.all_to_all(copies, "z", 0, 0, tiled=True), axis=0)


def lanes_of():
    return lax.broadcasted_iota(jnp.int32, (SUBLANES, LANES), 1)


def gram_kernel(filtered, applied, out, wide):
    size = filtered.shape[0]
    groups = size // SUBLANES
    spare = LANES - size
    full = groups - groups * spare // LANES
    lane = lanes_of()
    wide[...] = jnp.zeros(wide.shape, wide.dtype)
    contract = (((1,), (1,)), ((), ()))
    for half, source in enumerate((applied, filtered)):
        product = lax.dot_general(source[...], filtered[...], contract, preferred_element_type=jnp.float32)
        wide[half * size : (half + 1) * size, :size] = product

    def group_of(half, g):
        return wide[half * size + SUBLANES * g : half * size + SUBLANES * (g + 1), :]

    pieces = size // spare
    tiles = []
    for t in range(full):
        extra = group_of(0, full + t // pieces)
        tiles.append(jnp.where(lane < size, group_of(0, t), pltpu.roll(extra, size - spare * (t % pieces), 1)))
    for g in range(groups // 2):
        ends = SUBLANES * (g + 1)
        tiles.append(jnp.where(lane < ends, group_of(1, g), pltpu.roll(group_of(1, groups - 1 - g), ends, 1)))
    half_rows = out.shape[1]
    for t, tile in enumerate(tiles):
        out[2 * t] = tile[:half_rows]
        out[2 * t + 1] = tile[half_rows:]
    for rest in range(2 * len(tiles), out.shape[0]):
        out[rest] = jnp.zeros(out.shape[1:], out.dtype)


def packed_terms(filtered, applied, peers):
    size = filtered.shape[0]
    vmem = pl.BlockSpec(memory_space=pltpu.VMEM)
    return pl.pallas_call(
        gram_kernel,
        out_shape=jax.ShapeDtypeStruct((peers, SUBLANES // 2, LANES), jnp.float32),
        in_specs=[vmem, vmem],
        out_specs=vmem,
        scratch_shapes=[pltpu.VMEM((2 * size, LANES), jnp.float32)],
        compiler_params=pltpu.CompilerParams(vmem_limit_bytes=8 * 1024 * 1024),
        name="packed_terms",
    )(filtered, applied)


def total_over_all(partial):
    terms = lax.all_to_all(partial, LAYER, 0, 0, tiled=True)
    mine = summed_over_z(jnp.sum(terms, axis=0))
    return lax.all_to_all(jnp.broadcast_to(mine, partial.shape), LAYER, 0, 0, tiled=True)


def turn_kernel(scale, whole, filtered, inverse, crossed, turned, staged, square):
    size = inverse.shape[0]
    rows = turned.shape[2]
    groups = size // SUBLANES
    spare = LANES - size
    full = groups - groups * spare // LANES
    pieces = size // spare
    tile = (SUBLANES, LANES)
    sub = lax.broadcasted_iota(jnp.int32, tile, 0)
    lane = lanes_of()
    tiles = [jnp.concatenate([whole[2 * t], whole[2 * t + 1]], axis=0) for t in range(full + groups // 2)]

    for g in range(full):
        crossed[SUBLANES * g : SUBLANES * (g + 1), :] = tiles[g][:, :size]
    for g in range(full, groups):
        first = pieces * (g - full)
        value = pltpu.roll(tiles[first], spare, 1)
        for p in range(1, pieces):
            value = jnp.where(lane < spare * p, value, pltpu.roll(tiles[first + p], spare * (p + 1), 1))
        crossed[SUBLANES * g : SUBLANES * (g + 1), :] = value[:, :size]

    square[...] = jnp.zeros(square.shape, square.dtype)
    for g in range(groups // 2):
        ends = SUBLANES * (g + 1)
        last = groups - 1 - g
        square[SUBLANES * g : ends, :] = tiles[full + g]
        square[SUBLANES * last : SUBLANES * (last + 1), :] = pltpu.roll(tiles[full + g], LANES - ends, 1)
    mirrored = square[...].T
    left = [
        jnp.where(
            lane < SUBLANES * (g + 1),
            square[SUBLANES * g : SUBLANES * (g + 1), :],
            mirrored[SUBLANES * g : SUBLANES * (g + 1), :],
        )
        for g in range(groups)
    ]
    right = [jnp.where(lane == sub + SUBLANES * g, 1.0, 0.0) for g in range(groups)]

    def row_of(value, t):
        return jnp.broadcast_to(value[t : t + 1, :], tile)

    for b in range(groups):
        first = SUBLANES * b
        columns = [
            [jnp.broadcast_to(left[g][:, first + t : first + t + 1], tile) for g in range(b, groups)]
            for t in range(SUBLANES)
        ]
        diagonal = jnp.ones(tile, jnp.float32)
        for t in range(SUBLANES):
            pivot = row_of(columns[t][0], t)
            diagonal = jnp.where(sub == t, pivot, diagonal)
            part = 1.0 / pivot
            row_left = row_of(left[b], t) * part
            row_right = row_of(right[b], t) * part
            rest = range(t + 1, SUBLANES)
            row_columns = [row_of(columns[s][0], t) * part for s in rest]
            for g in range(b, groups):
                weight = columns[t][g - b]
                if g == b:
                    weight = jnp.where(sub > t, weight, 0.0)
                left[g] = left[g] - weight * row_left
                right[g] = right[g] - weight * row_right
                for s, row_column in zip(rest, row_columns):
                    columns[s][g - b] = columns[s][g - b] - weight * row_column
        inverse[first : first + SUBLANES, :] = (right[b] * lax.rsqrt(diagonal))[:, :size]

    rotation = inverse[...].astype(jnp.bfloat16)
    product = jnp.dot(rotation, filtered[...], preferred_element_type=jnp.float32) * scale
    width = turned.shape[3]
    for row in range(rows):
        staged[pl.ds(row, size, stride=rows), :] = product[:, row * width : (row + 1) * width]
    turned[...] = staged[...].reshape(turned.shape).astype(turned.dtype)


def inverse_and_turned(whole, filtered, scale, peers, rows):
    size = filtered.shape[0]
    width = filtered.shape[1] // rows
    vmem = pl.BlockSpec(memory_space=pltpu.VMEM)
    matrix = jax.ShapeDtypeStruct((size, size), jnp.float32)
    return pl.pallas_call(
        functools.partial(turn_kernel, scale),
        out_shape=(matrix, matrix, jax.ShapeDtypeStruct((peers, size // peers, rows, width), jnp.bfloat16)),
        in_specs=[vmem, vmem],
        out_specs=(vmem, vmem, vmem),
        scratch_shapes=[pltpu.VMEM((size * rows, width), jnp.float32), pltpu.VMEM((LANES, LANES), jnp.float32)],
        compiler_params=pltpu.CompilerParams(vmem_limit_bytes=8 * 1024 * 1024),
        name="inverse_and_turned",
    )(whole, filtered)


def projection(inverse, cross):
    return jnp.dot(
        jnp.dot(inverse, cross, precision=lax.Precision.HIGHEST),
        inverse.T,
        precision=lax.Precision.HIGHEST,
    )


def per_device(initial_block, labels, filter_low, filter_high):
    share, _, height, width = initial_block.shape
    group, blocks = lax.axis_size(GROUP), lax.axis_size(MODE)
    local = share // group
    modes = share * blocks
    rows = height // blocks
    scale = math.sqrt(height * width * group * lax.axis_size("z"))

    own = lax.all_to_all(packed(initial_block, labels, group), GROUP, 0, 0, tiled=True)
    extra = REACH - group
    lo, hi = shifted(own, "z", 1), shifted(own, "z", -1)
    far_lo, far_hi = shifted(own[group - extra :], "z", 2), shifted(own[:extra], "z", -2)

    bounds = jnp.stack([filter_low, filter_high])
    pair = filtered_and_applied(bounds, far_lo, lo, own, hi, far_hi, blocks)
    pair = pair.reshape(blocks * group, 2 * local, rows, width)

    pair = lax.all_to_all(pair, LAYER, 0, 0, tiled=True)
    filtered = pair[:, :local].reshape(modes, rows * width)
    applied = pair[:, local:].reshape(modes, rows * width)
    total = total_over_all(packed_terms(filtered, applied, blocks * group))
    inverse, crossed, turned = inverse_and_turned(total, filtered, scale, blocks, rows)
    projected = projection(inverse, crossed.T)
    turned = lax.all_to_all(turned, MODE, 0, 0, tiled=True)
    modes_out = jnp.transpose(turned, (1, 0, 2, 3)).reshape(share, 1, height, width)
    return (modes_out, projected)


def solution(mesh):
    devices = mesh.devices
    slabs, modes = devices.shape
    fine = Mesh(devices.reshape(slabs // 4, 2, 2, 2, modes // 2), AXES)
    placed = (P(MODE, ("z",) + GROUP, None, None), P(("z",) + GROUP, None, None), P(), P())
    return jax.shard_map(
        per_device,
        mesh=fine,
        in_specs=placed,
        out_specs=(P(MODE, ("z",) + GROUP, None, None), P()),
        check_vma=False,
    )
```

```python
import functools
import math

import jax
import jax.numpy as jnp
from jax import lax
from jax.experimental import pallas as pl
from jax.experimental.pallas import tpu as pltpu
from jax.sharding import Mesh, PartitionSpec as P

DEGREE = 4
ROOTS = (0.0, 0.7745967, 1.0, 1.3416408)
REACH = DEGREE + 1
SUBLANES, LANES = 8, 128
UNROLL = 4

AXES = ("z", "xl", "core", "xh", "y")
GROUP = ("xl", "core")
MODE = ("xh", "y")
LAYER = ("xh", "y", "xl", "core")


def root_of(label):
    root = jnp.where(label == 1.0, ROOTS[1], 0.0)
    root = jnp.where(label == 2.0, ROOTS[2], root)
    return jnp.where(label == 3.0, ROOTS[3], root)


def filter_kernel(bounds, lo, own, hi, out, short, share, even, odd, weak_even, weak_odd, strong, degree):
    planes, height, width = degree.shape
    local = even.shape[1]
    rows = out.shape[3]
    low, high = bounds[0], bounds[1]
    centre = 0.5 * (high + low)
    scale = 1.0 / (0.5 * (high - low))
    inner = pl.ds(SUBLANES, height)
    lane = lax.broadcasted_iota(jnp.int32, (height, width), 1)

    def beside(ref, *index):
        value = ref[(*index, inner)]
        up = ref[(*index, pl.ds(SUBLANES - 1, height))]
        down = ref[(*index, pl.ds(SUBLANES + 1, height))]
        left = jnp.where(lane == 0, 0.0, pltpu.roll(value, 1, 1))
        right = jnp.where(lane == width - 1, 0.0, pltpu.roll(value, width - 1, 1))
        return value, (up + down) + (left + right)

    edge = jnp.zeros((SUBLANES, width), jnp.float32)

    def clear(plane, carry):
        for first in (0, SUBLANES + height):
            strong[plane, pl.ds(first, SUBLANES)] = edge
            for mode in range(local):
                weak_even[plane, mode, pl.ds(first, SUBLANES)] = edge
                weak_odd[plane, mode, pl.ds(first, SUBLANES)] = edge
        return carry

    lax.fori_loop(0, planes, clear, 0)

    depth = own.shape[0]
    for plane in (0, planes - 1):
        strong[plane, inner] = jnp.zeros((height, width), jnp.float32)
        even[plane] = jnp.zeros(even.shape[1:], jnp.float32)
        for mode in range(local):
            weak_even[plane, mode, inner] = jnp.zeros((height, width), jnp.float32)

    for source, start in ((lo, REACH - depth), (own, REACH), (hi, REACH + depth)):
        count = source.shape[0]

        def load(index, carry, source=source, start=start):
            label = source[index, local].astype(jnp.float32)
            root = root_of(label)
            strong[start + index, inner] = root
            for mode in range(local):
                value = jnp.where(label > 0.0, source[index, mode].astype(jnp.float32), 0.0)
                even[start + index, mode] = value
                weak_even[start + index, mode, inner] = root * value
            return carry

        lax.fori_loop(0, count, load, 0, unroll=min(count, UNROLL))

    def weigh(plane, carry):
        root, around = beside(strong, plane)
        degree[plane] = root * (strong[plane - 1, inner] + strong[plane + 1, inner] + around)
        return carry

    lax.fori_loop(1, planes - 1, weigh, 0, unroll=UNROLL)

    cur, prev, weak, weak_next = even, odd, weak_even, weak_odd
    for step in range(DEGREE):
        factor = scale if step == 0 else 2.0 * scale

        def advance(plane, carry, cur=cur, prev=prev, weak=weak, weak_next=weak_next, factor=factor, step=step):
            root = strong[plane, inner]
            here = (degree[plane] - centre) * factor
            there = root * factor
            for mode in range(local):
                _, around = beside(weak, plane, mode)
                around = around + (weak[plane - 1, mode, inner] + weak[plane + 1, mode, inner])
                value = here * cur[plane, mode] - there * around
                if step > 0:
                    value = value - prev[plane, mode]
                prev[plane, mode] = value
                weak_next[plane, mode, inner] = root * value
            return carry

        lax.fori_loop(step + 1, planes - step - 1, advance, 0, unroll=UNROLL)
        cur, prev = prev, cur
        weak, weak_next = weak_next, weak

    for index in range(depth):
        plane = REACH + index
        root, heavy = strong[plane, inner], degree[plane]
        for mode in range(local):
            value = cur[plane, mode]
            _, around = beside(weak, plane, mode)
            around = around + (weak[plane - 1, mode, inner] + weak[plane + 1, mode, inner])
            image = heavy * value - root * around
            out[:, index, mode] = value.reshape(-1, rows, width).astype(out.dtype)
            if index == 0:
                short[0, mode] = image
            elif index == depth - 1:
                short[1, mode] = image
            else:
                out[:, index, local + mode] = image.reshape(-1, rows, width).astype(out.dtype)

    for side, (outer, step) in enumerate(((REACH - depth, 1), (planes - 1 - REACH + depth, -1))):
        between = strong[outer + step * (DEGREE - 1), inner]
        for index in range(DEGREE - 1):
            between = between * strong[outer + step * index, inner]
        share[side] = (8.0 * scale * scale * scale * scale) * (between * between) * strong[outer + step * DEGREE, inner]


def finish_kernel(lo, hi, far_lo, far_hi, short, share, done, out):
    out[...] = done[...]
    local = short.shape[1]
    depth, rows, width = out.shape[1], out.shape[3], out.shape[4]
    sides = ((lo, 0, far_lo, 0, 0), (hi, depth - 1, far_hi, 0, depth - 1))
    for side, (near, near_plane, far, far_plane, index) in enumerate(sides):
        weight = share[side] * root_of(far[far_plane, local].astype(jnp.float32))
        for mode in range(local):
            jump = near[near_plane, mode].astype(jnp.float32) - far[far_plane, mode].astype(jnp.float32)
            image = short[side, mode] + weight * jump
            out[:, index, local + mode] = image.reshape(-1, rows, width).astype(out.dtype)


def filtered_and_applied(bounds, far_lo, lo, own, hi, far_hi, blocks):
    depth, fields, height, width = own.shape
    local = fields - 1
    planes = depth + 2 * REACH
    field = pltpu.VMEM((planes, local, height, width), jnp.float32)
    rimmed = pltpu.VMEM((planes, local, height + 2 * SUBLANES, width), jnp.float32)
    root = pltpu.VMEM((planes, height + 2 * SUBLANES, width), jnp.float32)
    degree = pltpu.VMEM((planes, height, width), jnp.float32)
    vmem = pl.BlockSpec(memory_space=pltpu.VMEM)
    whole = jax.ShapeDtypeStruct((blocks, depth, 2 * local, height // blocks, width), jnp.bfloat16)
    steps = planes * local * height * width
    whole_part, short, share = pl.pallas_call(
        filter_kernel,
        out_shape=(
            whole,
            jax.ShapeDtypeStruct((2, local, height, width), jnp.float32),
            jax.ShapeDtypeStruct((2, height, width), jnp.float32),
        ),
        in_specs=[pl.BlockSpec(memory_space=pltpu.SMEM)] + [vmem] * 3,
        out_specs=(vmem,) * 3,
        scratch_shapes=[field, field, rimmed, rimmed, root, degree],
        compiler_params=pltpu.CompilerParams(vmem_limit_bytes=40 * 1024 * 1024),
        cost_estimate=pl.CostEstimate(flops=100 * steps, bytes_accessed=8 * steps, transcendentals=0),
        name="chebyshev_filter",
    )(bounds, lo, own, hi)
    return pl.pallas_call(
        finish_kernel,
        out_shape=whole,
        in_specs=[vmem] * 7,
        out_specs=vmem,
        compiler_params=pltpu.CompilerParams(vmem_limit_bytes=8 * 1024 * 1024),
        name="outermost_planes",
    )(lo, hi, far_lo, far_hi, short, share, whole_part)


def pack_kernel(block, labels, out):
    group, fields = out.shape[:2]
    local = fields - 1
    tags = labels[0].astype(jnp.float32).astype(out.dtype)
    for peer in range(group):
        for mode in range(local):
            out[peer, mode] = block[peer * local + mode, 0]
        out[peer, local] = tags


def packed(block, labels, group):
    share, _, height, width = block.shape
    vmem = pl.BlockSpec(memory_space=pltpu.VMEM)
    return pl.pallas_call(
        pack_kernel,
        out_shape=jax.ShapeDtypeStruct((group, share // group + 1, height, width), block.dtype),
        in_specs=[vmem, vmem],
        out_specs=vmem,
        name="pack",
    )(block, labels)


def shifted(value, axis, step):
    size = lax.axis_size(axis)
    pairs = [(i, i + step) for i in range(size) if 0 <= i + step < size]
    return lax.ppermute(value, axis, pairs)


def summed_over_z(value):
    copies = jnp.broadcast_to(value, (lax.axis_size("z"),) + value.shape)
    return jnp.sum(lax.all_to_all(copies, "z", 0, 0, tiled=True), axis=0)


def lanes_of():
    return lax.broadcasted_iota(jnp.int32, (SUBLANES, LANES), 1)


def gram_kernel(filtered, applied, out, wide):
    size = filtered.shape[0]
    groups = size // SUBLANES
    spare = LANES - size
    full = groups - groups * spare // LANES
    lane = lanes_of()
    wide[...] = jnp.zeros(wide.shape, wide.dtype)
    contract = (((1,), (1,)), ((), ()))
    for half, source in enumerate((applied, filtered)):
        product = lax.dot_general(source[...], filtered[...], contract, preferred_element_type=jnp.float32)
        wide[half * size : (half + 1) * size, :size] = product

    def group_of(half, g):
        return wide[half * size + SUBLANES * g : half * size + SUBLANES * (g + 1), :]

    pieces = size // spare
    tiles = []
    for t in range(full):
        extra = group_of(0, full + t // pieces)
        tiles.append(jnp.where(lane < size, group_of(0, t), pltpu.roll(extra, size - spare * (t % pieces), 1)))
    for g in range(groups // 2):
        ends = SUBLANES * (g + 1)
        tiles.append(jnp.where(lane < ends, group_of(1, g), pltpu.roll(group_of(1, groups - 1 - g), ends, 1)))
    half_rows = out.shape[1]
    for t, tile in enumerate(tiles):
        out[2 * t] = tile[:half_rows]
        out[2 * t + 1] = tile[half_rows:]
    for rest in range(2 * len(tiles), out.shape[0]):
        out[rest] = jnp.zeros(out.shape[1:], out.dtype)


def packed_terms(filtered, applied, peers):
    size = filtered.shape[0]
    vmem = pl.BlockSpec(memory_space=pltpu.VMEM)
    return pl.pallas_call(
        gram_kernel,
        out_shape=jax.ShapeDtypeStruct((peers, SUBLANES // 2, LANES), jnp.float32),
        in_specs=[vmem, vmem],
        out_specs=vmem,
        scratch_shapes=[pltpu.VMEM((2 * size, LANES), jnp.float32)],
        compiler_params=pltpu.CompilerParams(vmem_limit_bytes=8 * 1024 * 1024),
        name="packed_terms",
    )(filtered, applied)


def total_over_all(partial):
    terms = lax.all_to_all(partial, LAYER, 0, 0, tiled=True)
    mine = summed_over_z(jnp.sum(terms, axis=0))
    return lax.all_to_all(jnp.broadcast_to(mine, partial.shape), LAYER, 0, 0, tiled=True)


def turn_kernel(scale, whole, filtered, inverse, crossed, turned, staged, square):
    size = inverse.shape[0]
    rows = turned.shape[2]
    groups = size // SUBLANES
    spare = LANES - size
    full = groups - groups * spare // LANES
    pieces = size // spare
    tile = (SUBLANES, LANES)
    sub = lax.broadcasted_iota(jnp.int32, tile, 0)
    lane = lanes_of()
    tiles = [jnp.concatenate([whole[2 * t], whole[2 * t + 1]], axis=0) for t in range(full + groups // 2)]

    for g in range(full):
        crossed[SUBLANES * g : SUBLANES * (g + 1), :] = tiles[g][:, :size]
    for g in range(full, groups):
        first = pieces * (g - full)
        value = pltpu.roll(tiles[first], spare, 1)
        for p in range(1, pieces):
            value = jnp.where(lane < spare * p, value, pltpu.roll(tiles[first + p], spare * (p + 1), 1))
        crossed[SUBLANES * g : SUBLANES * (g + 1), :] = value[:, :size]

    square[...] = jnp.zeros(square.shape, square.dtype)
    for g in range(groups // 2):
        ends = SUBLANES * (g + 1)
        last = groups - 1 - g
        square[SUBLANES * g : ends, :] = tiles[full + g]
        square[SUBLANES * last : SUBLANES * (last + 1), :] = pltpu.roll(tiles[full + g], LANES - ends, 1)
    mirrored = square[...].T
    left = [
        jnp.where(
            lane < SUBLANES * (g + 1),
            square[SUBLANES * g : SUBLANES * (g + 1), :],
            mirrored[SUBLANES * g : SUBLANES * (g + 1), :],
        )
        for g in range(groups)
    ]
    right = [jnp.where(lane == sub + SUBLANES * g, 1.0, 0.0) for g in range(groups)]

    def row_of(value, t):
        return jnp.broadcast_to(value[t : t + 1, :], tile)

    for b in range(groups):
        first = SUBLANES * b
        columns = [
            [jnp.broadcast_to(left[g][:, first + t : first + t + 1], tile) for g in range(b, groups)]
            for t in range(SUBLANES)
        ]
        diagonal = jnp.ones(tile, jnp.float32)
        for t in range(SUBLANES):
            pivot = row_of(columns[t][0], t)
            diagonal = jnp.where(sub == t, pivot, diagonal)
            part = 1.0 / pivot
            row_left = row_of(left[b], t) * part
            row_right = row_of(right[b], t) * part
            rest = range(t + 1, SUBLANES)
            row_columns = [row_of(columns[s][0], t) * part for s in rest]
            for g in range(b, groups):
                weight = columns[t][g - b]
                if g == b:
                    weight = jnp.where(sub > t, weight, 0.0)
                left[g] = left[g] - weight * row_left
                right[g] = right[g] - weight * row_right
                for s, row_column in zip(rest, row_columns):
                    columns[s][g - b] = columns[s][g - b] - weight * row_column
        inverse[first : first + SUBLANES, :] = (right[b] * lax.rsqrt(diagonal))[:, :size]

    rotation = inverse[...].astype(jnp.bfloat16)
    product = jnp.dot(rotation, filtered[...], preferred_element_type=jnp.float32) * scale
    width = turned.shape[3]
    for row in range(rows):
        staged[pl.ds(row, size, stride=rows), :] = product[:, row * width : (row + 1) * width]
    turned[...] = staged[...].reshape(turned.shape).astype(turned.dtype)


def inverse_and_turned(whole, filtered, scale, peers, rows):
    size = filtered.shape[0]
    width = filtered.shape[1] // rows
    vmem = pl.BlockSpec(memory_space=pltpu.VMEM)
    matrix = jax.ShapeDtypeStruct((size, size), jnp.float32)
    return pl.pallas_call(
        functools.partial(turn_kernel, scale),
        out_shape=(matrix, matrix, jax.ShapeDtypeStruct((peers, size // peers, rows, width), jnp.bfloat16)),
        in_specs=[vmem, vmem],
        out_specs=(vmem, vmem, vmem),
        scratch_shapes=[pltpu.VMEM((size * rows, width), jnp.float32), pltpu.VMEM((LANES, LANES), jnp.float32)],
        compiler_params=pltpu.CompilerParams(vmem_limit_bytes=8 * 1024 * 1024),
        name="inverse_and_turned",
    )(whole, filtered)


def projection(inverse, cross):
    return jnp.dot(
        jnp.dot(inverse, cross, precision=lax.Precision.HIGHEST),
        inverse.T,
        precision=lax.Precision.HIGHEST,
    )


def per_device(initial_block, labels, filter_low, filter_high):
    share, _, height, width = initial_block.shape
    group, blocks = lax.axis_size(GROUP), lax.axis_size(MODE)
    local = share // group
    modes = share * blocks
    rows = height // blocks
    scale = math.sqrt(height * width * group * lax.axis_size("z"))

    own = lax.all_to_all(packed(initial_block, labels, group), GROUP, 0, 0, tiled=True)
    extra = REACH - group
    lo, hi = shifted(own, "z", 1), shifted(own, "z", -1)
    far_lo, far_hi = shifted(own[group - extra :], "z", 2), shifted(own[:extra], "z", -2)

    bounds = jnp.stack([filter_low, filter_high])
    pair = filtered_and_applied(bounds, far_lo, lo, own, hi, far_hi, blocks)
    pair = pair.reshape(blocks * group, 2 * local, rows, width)

    pair = lax.all_to_all(pair, LAYER, 0, 0, tiled=True)
    filtered = pair[:, :local].reshape(modes, rows * width)
    applied = pair[:, local:].reshape(modes, rows * width)
    total = total_over_all(packed_terms(filtered, applied, blocks * group))
    inverse, crossed, turned = inverse_and_turned(total, filtered, scale, blocks, rows)
    projected = projection(inverse, crossed.T)
    turned = lax.all_to_all(turned, MODE, 0, 0, tiled=True)
    modes_out = jnp.transpose(turned, (1, 0, 2, 3)).reshape(share, 1, height, width)
    return (modes_out, projected)


def solution(mesh):
    devices = mesh.devices
    slabs, modes = devices.shape
    fine = Mesh(devices.reshape(slabs // 4, 2, 2, 2, modes // 2), AXES)
    placed = (P(MODE, ("z",) + GROUP, None, None), P(("z",) + GROUP, None, None), P(), P())
    return jax.shard_map(
        per_device,
        mesh=fine,
        in_specs=placed,
        out_specs=(P(MODE, ("z",) + GROUP, None, None), P()),
        check_vma=False,
    )
```

```python
import functools
import math

import jax
import jax.numpy as jnp
from jax import lax
from jax.experimental import pallas as pl
from jax.experimental.pallas import tpu as pltpu
from jax.sharding import Mesh, PartitionSpec as P

DEGREE = 4
ROOTS = (0.0, 0.7745967, 1.0, 1.3416408)
REACH = DEGREE + 1
SUBLANES, LANES = 8, 128
UNROLL = 6

AXES = ("z", "xl", "core", "xh", "y")
GROUP = ("xl", "core")
MODE = ("xh", "y")
LAYER = ("xh", "y", "xl", "core")


def root_of(label):
    root = jnp.where(label == 1.0, ROOTS[1], 0.0)
    root = jnp.where(label == 2.0, ROOTS[2], root)
    return jnp.where(label == 3.0, ROOTS[3], root)


def inverse_root_of(label):
    value = jnp.where(label == 1.0, 1.0 / ROOTS[1], 0.0)
    value = jnp.where(label == 2.0, 1.0 / ROOTS[2], value)
    return jnp.where(label == 3.0, 1.0 / ROOTS[3], value)


def filter_kernel(lowest, highest, lo, own, hi, out, short, share, even, odd, strong, square, degree):
    planes, height, width = degree.shape
    local = even.shape[1]
    rows = out.shape[3]
    depth = own.shape[0]
    low, high = lowest[0], highest[0]
    centre = 0.5 * (high + low)
    scale = 1.0 / (0.5 * (high - low))
    inner = pl.ds(SUBLANES, height)
    lane = lax.broadcasted_iota(jnp.int32, (height, width), 1)

    def beside(ref, plane, *index):
        value = ref[(plane, *index, inner)]
        up = ref[(plane, *index, pl.ds(SUBLANES - 1, height))]
        down = ref[(plane, *index, pl.ds(SUBLANES + 1, height))]
        left = jnp.where(lane == 0, 0.0, pltpu.roll(value, 1, 1))
        right = jnp.where(lane == width - 1, 0.0, pltpu.roll(value, width - 1, 1))
        before, after = ref[(plane - 1, *index, inner)], ref[(plane + 1, *index, inner)]
        return value, (up + down) + (left + right) + (before + after)

    edge = jnp.zeros((SUBLANES, width), jnp.float32)

    def clear(plane, carry):
        for first in (0, SUBLANES + height):
            strong[plane, pl.ds(first, SUBLANES)] = edge
            for mode in range(local):
                even[plane, mode, pl.ds(first, SUBLANES)] = edge
                odd[plane, mode, pl.ds(first, SUBLANES)] = edge
        return carry

    lax.fori_loop(0, planes, clear, 0)

    for plane in (0, planes - 1):
        strong[plane, inner] = jnp.zeros((height, width), jnp.float32)
        for mode in range(local):
            even[plane, mode, inner] = jnp.zeros((height, width), jnp.float32)

    for source, start in ((lo, REACH - depth), (own, REACH), (hi, REACH + depth)):

        def load(index, carry, source=source, start=start):
            root = root_of(source[index, local].astype(jnp.float32))
            strong[start + index, inner] = root
            square[start + index] = root * root
            for mode in range(local):
                even[start + index, mode, inner] = root * source[index, mode].astype(jnp.float32)
            return carry

        lax.fori_loop(0, depth, load, 0, unroll=min(depth, UNROLL))

    def weigh(plane, carry):
        root, around = beside(strong, plane)
        degree[plane] = root * around
        return carry

    lax.fori_loop(1, planes - 1, weigh, 0, unroll=UNROLL)

    cur, prev = even, odd
    for step in range(DEGREE):
        factor = scale if step == 0 else 2.0 * scale

        def advance(plane, carry, cur=cur, prev=prev, factor=factor, step=step):
            here = (degree[plane] - centre) * factor
            there = square[plane] * factor
            for mode in range(local):
                value, around = beside(cur, plane, mode)
                value = here * value - there * around
                if step > 0:
                    value = value - prev[plane, mode, inner]
                prev[plane, mode, inner] = value
            return carry

        lax.fori_loop(step + 1, planes - step - 1, advance, 0, unroll=UNROLL)
        cur, prev = prev, cur

    for index in range(depth):
        plane = REACH + index
        heavy, weight = degree[plane], square[plane]
        upright = inverse_root_of(own[index, local].astype(jnp.float32))
        for mode in range(local):
            value, around = beside(cur, plane, mode)
            image = upright * (heavy * value - weight * around)
            out[:, index, mode] = (upright * value).reshape(-1, rows, width).astype(out.dtype)
            if index == 0:
                short[0, mode] = image
            elif index == depth - 1:
                short[1, mode] = image
            else:
                out[:, index, local + mode] = image.reshape(-1, rows, width).astype(out.dtype)

    for side, (outer, step) in enumerate(((REACH - depth, 1), (planes - 1 - REACH + depth, -1))):
        between = square[outer]
        for index in range(1, DEGREE):
            between = between * square[outer + step * index]
        share[side] = (8.0 * scale * scale * scale * scale) * between * strong[outer + step * DEGREE, inner]


def finish_kernel(lo, hi, far_lo, far_hi, short, share, done, out):
    out[...] = done[...]
    local = short.shape[1]
    depth, rows, width = out.shape[1], out.shape[3], out.shape[4]
    sides = ((lo, 0, far_lo, 0, 0), (hi, depth - 1, far_hi, 0, depth - 1))
    for side, (near, near_plane, far, far_plane, index) in enumerate(sides):
        weight = share[side] * root_of(far[far_plane, local].astype(jnp.float32))
        for mode in range(local):
            jump = near[near_plane, mode].astype(jnp.float32) - far[far_plane, mode].astype(jnp.float32)
            image = short[side, mode] + weight * jump
            out[:, index, local + mode] = image.reshape(-1, rows, width).astype(out.dtype)


def filtered_and_applied(lowest, highest, far_lo, lo, own, hi, far_hi, blocks):
    depth, fields, height, width = own.shape
    local = fields - 1
    planes = depth + 2 * REACH
    rimmed = pltpu.VMEM((planes, local, height + 2 * SUBLANES, width), jnp.float32)
    root = pltpu.VMEM((planes, height + 2 * SUBLANES, width), jnp.float32)
    flat = pltpu.VMEM((planes, height, width), jnp.float32)
    vmem = pl.BlockSpec(memory_space=pltpu.VMEM)
    whole = jax.ShapeDtypeStruct((blocks, depth, 2 * local, height // blocks, width), jnp.bfloat16)
    steps = planes * local * height * width
    whole_part, short, share = pl.pallas_call(
        filter_kernel,
        out_shape=(
            whole,
            jax.ShapeDtypeStruct((2, local, height, width), jnp.float32),
            jax.ShapeDtypeStruct((2, height, width), jnp.float32),
        ),
        in_specs=[pl.BlockSpec(memory_space=pltpu.SMEM)] * 2 + [vmem] * 3,
        out_specs=(vmem,) * 3,
        scratch_shapes=[rimmed, rimmed, root, flat, flat],
        compiler_params=pltpu.CompilerParams(vmem_limit_bytes=40 * 1024 * 1024),
        cost_estimate=pl.CostEstimate(flops=100 * steps, bytes_accessed=8 * steps, transcendentals=0),
        name="chebyshev_filter",
    )(lowest, highest, lo, own, hi)
    return pl.pallas_call(
        finish_kernel,
        out_shape=whole,
        in_specs=[vmem] * 7,
        out_specs=vmem,
        compiler_params=pltpu.CompilerParams(vmem_limit_bytes=8 * 1024 * 1024),
        name="outermost_planes",
    )(lo, hi, far_lo, far_hi, short, share, whole_part)


def pack_kernel(block, labels, out):
    group, fields = out.shape[:2]
    local = fields - 1
    tags = labels[0].astype(jnp.float32).astype(out.dtype)
    for peer in range(group):
        for mode in range(local):
            out[peer, mode] = block[peer * local + mode, 0]
        out[peer, local] = tags


def packed(block, labels, group):
    share, _, height, width = block.shape
    vmem = pl.BlockSpec(memory_space=pltpu.VMEM)
    return pl.pallas_call(
        pack_kernel,
        out_shape=jax.ShapeDtypeStruct((group, share // group + 1, height, width), block.dtype),
        in_specs=[vmem, vmem],
        out_specs=vmem,
        compiler_params=pltpu.CompilerParams(vmem_limit_bytes=8 * 1024 * 1024),
        name="pack",
    )(block, labels)


def shifted(value, axis, step):
    size = lax.axis_size(axis)
    pairs = [(i, i + step) for i in range(size) if 0 <= i + step < size]
    return lax.ppermute(value, axis, pairs)


def summed_over_z(value):
    copies = jnp.broadcast_to(value, (lax.axis_size("z"),) + value.shape)
    return jnp.sum(lax.all_to_all(copies, "z", 0, 0, tiled=True), axis=0)


def lanes_of():
    return lax.broadcasted_iota(jnp.int32, (SUBLANES, LANES), 1)


def gram_kernel(filtered, applied, out, wide):
    size = filtered.shape[0]
    groups = size // SUBLANES
    spare = LANES - size
    full = groups - groups * spare // LANES
    lane = lanes_of()
    wide[...] = jnp.zeros(wide.shape, wide.dtype)
    contract = (((1,), (1,)), ((), ()))
    for half, source in enumerate((applied, filtered)):
        product = lax.dot_general(source[...], filtered[...], contract, preferred_element_type=jnp.float32)
        wide[half * size : (half + 1) * size, :size] = product

    def group_of(half, g):
        return wide[half * size + SUBLANES * g : half * size + SUBLANES * (g + 1), :]

    pieces = size // spare
    tiles = []
    for t in range(full):
        extra = group_of(0, full + t // pieces)
        tiles.append(jnp.where(lane < size, group_of(0, t), pltpu.roll(extra, size - spare * (t % pieces), 1)))
    for g in range(groups // 2):
        ends = SUBLANES * (g + 1)
        tiles.append(jnp.where(lane < ends, group_of(1, g), pltpu.roll(group_of(1, groups - 1 - g), ends, 1)))
    half_rows = out.shape[1]
    for t, tile in enumerate(tiles):
        out[2 * t] = tile[:half_rows]
        out[2 * t + 1] = tile[half_rows:]
    for rest in range(2 * len(tiles), out.shape[0]):
        out[rest] = jnp.zeros(out.shape[1:], out.dtype)


def packed_terms(filtered, applied, peers):
    size = filtered.shape[0]
    vmem = pl.BlockSpec(memory_space=pltpu.VMEM)
    return pl.pallas_call(
        gram_kernel,
        out_shape=jax.ShapeDtypeStruct((peers, SUBLANES // 2, LANES), jnp.float32),
        in_specs=[vmem, vmem],
        out_specs=vmem,
        scratch_shapes=[pltpu.VMEM((2 * size, LANES), jnp.float32)],
        compiler_params=pltpu.CompilerParams(vmem_limit_bytes=8 * 1024 * 1024),
        name="packed_terms",
    )(filtered, applied)


def total_over_all(partial):
    terms = lax.all_to_all(partial, LAYER, 0, 0, tiled=True)
    mine = summed_over_z(jnp.sum(terms, axis=0))
    return lax.all_to_all(jnp.broadcast_to(mine, partial.shape), LAYER, 0, 0, tiled=True)


def turn_kernel(scale, whole, filtered, inverse, crossed, turned, staged, square):
    size = inverse.shape[0]
    rows = turned.shape[2]
    groups = size // SUBLANES
    spare = LANES - size
    full = groups - groups * spare // LANES
    pieces = size // spare
    tile = (SUBLANES, LANES)
    sub = lax.broadcasted_iota(jnp.int32, tile, 0)
    lane = lanes_of()
    tiles = [jnp.concatenate([whole[2 * t], whole[2 * t + 1]], axis=0) for t in range(full + groups // 2)]

    for g in range(full):
        crossed[SUBLANES * g : SUBLANES * (g + 1), :] = tiles[g][:, :size]
    for g in range(full, groups):
        first = pieces * (g - full)
        value = pltpu.roll(tiles[first], spare, 1)
        for p in range(1, pieces):
            value = jnp.where(lane < spare * p, value, pltpu.roll(tiles[first + p], spare * (p + 1), 1))
        crossed[SUBLANES * g : SUBLANES * (g + 1), :] = value[:, :size]

    square[...] = jnp.zeros(square.shape, square.dtype)
    for g in range(groups // 2):
        ends = SUBLANES * (g + 1)
        last = groups - 1 - g
        square[SUBLANES * g : ends, :] = tiles[full + g]
        square[SUBLANES * last : SUBLANES * (last + 1), :] = pltpu.roll(tiles[full + g], LANES - ends, 1)
    mirrored = square[...].T
    left = [
        jnp.where(
            lane < SUBLANES * (g + 1),
            square[SUBLANES * g : SUBLANES * (g + 1), :],
            mirrored[SUBLANES * g : SUBLANES * (g + 1), :],
        )
        for g in range(groups)
    ]
    right = [jnp.where(lane == sub + SUBLANES * g, 1.0, 0.0) for g in range(groups)]

    def row_of(value, t):
        return jnp.broadcast_to(value[t : t + 1, :], tile)

    for b in range(groups):
        first = SUBLANES * b
        columns = [
            [jnp.broadcast_to(left[g][:, first + t : first + t + 1], tile) for g in range(b, groups)]
            for t in range(SUBLANES)
        ]
        diagonal = jnp.ones(tile, jnp.float32)
        for t in range(SUBLANES):
            pivot = row_of(columns[t][0], t)
            diagonal = jnp.where(sub == t, pivot, diagonal)
            part = 1.0 / pivot
            row_left = row_of(left[b], t) * part
            row_right = row_of(right[b], t) * part
            rest = range(t + 1, SUBLANES)
            row_columns = [row_of(columns[s][0], t) * part for s in rest]
            for g in range(b, groups):
                weight = columns[t][g - b]
                if g == b:
                    weight = jnp.where(sub > t, weight, 0.0)
                left[g] = left[g] - weight * row_left
                right[g] = right[g] - weight * row_right
                for s, row_column in zip(rest, row_columns):
                    columns[s][g - b] = columns[s][g - b] - weight * row_column
        inverse[first : first + SUBLANES, :] = (right[b] * lax.rsqrt(diagonal))[:, :size]

    rotation = inverse[...].astype(jnp.bfloat16)
    product = jnp.dot(rotation, filtered[...], preferred_element_type=jnp.float32) * scale
    width = turned.shape[3]
    for row in range(rows):
        staged[pl.ds(row, size, stride=rows), :] = product[:, row * width : (row + 1) * width]
    turned[...] = staged[...].reshape(turned.shape).astype(turned.dtype)


def inverse_and_turned(whole, filtered, scale, peers, rows):
    size = filtered.shape[0]
    width = filtered.shape[1] // rows
    vmem = pl.BlockSpec(memory_space=pltpu.VMEM)
    matrix = jax.ShapeDtypeStruct((size, size), jnp.float32)
    return pl.pallas_call(
        functools.partial(turn_kernel, scale),
        out_shape=(matrix, matrix, jax.ShapeDtypeStruct((peers, size // peers, rows, width), jnp.bfloat16)),
        in_specs=[vmem, vmem],
        out_specs=(vmem, vmem, vmem),
        scratch_shapes=[pltpu.VMEM((size * rows, width), jnp.float32), pltpu.VMEM((LANES, LANES), jnp.float32)],
        compiler_params=pltpu.CompilerParams(vmem_limit_bytes=8 * 1024 * 1024),
        name="inverse_and_turned",
    )(whole, filtered)


def projection(inverse, cross):
    return jnp.dot(
        jnp.dot(inverse, cross, precision=lax.Precision.HIGHEST),
        inverse.T,
        precision=lax.Precision.HIGHEST,
    )


def per_device(initial_block, labels, filter_low, filter_high):
    share, _, height, width = initial_block.shape
    group, blocks = lax.axis_size(GROUP), lax.axis_size(MODE)
    local = share // group
    modes = share * blocks
    rows = height // blocks
    scale = math.sqrt(height * width * group * lax.axis_size("z"))

    own = lax.all_to_all(packed(initial_block, labels, group), GROUP, 0, 0, tiled=True)
    extra = REACH - group
    lo, hi = shifted(own, "z", 1), shifted(own, "z", -1)
    far_lo, far_hi = shifted(own[group - extra :], "z", 2), shifted(own[:extra], "z", -2)

    lowest, highest = jnp.reshape(filter_low, (1,)), jnp.reshape(filter_high, (1,))
    pair = filtered_and_applied(lowest, highest, far_lo, lo, own, hi, far_hi, blocks)
    pair = pair.reshape(blocks * group, 2 * local, rows, width)

    pair = lax.all_to_all(pair, LAYER, 0, 0, tiled=True)
    filtered = pair[:, :local].reshape(modes, rows * width)
    applied = pair[:, local:].reshape(modes, rows * width)
    total = total_over_all(packed_terms(filtered, applied, blocks * group))
    inverse, crossed, turned = inverse_and_turned(total, filtered, scale, blocks, rows)
    projected = projection(inverse, crossed.T)
    turned = lax.all_to_all(turned, MODE, 0, 0, tiled=True)
    modes_out = jnp.transpose(turned, (1, 0, 2, 3)).reshape(share, 1, height, width)
    return (modes_out, projected)


def solution(mesh):
    devices = mesh.devices
    slabs, modes = devices.shape
    fine = Mesh(devices.reshape(slabs // 4, 2, 2, 2, modes // 2), AXES)
    placed = (P(MODE, ("z",) + GROUP, None, None), P(("z",) + GROUP, None, None), P(), P())
    return jax.shard_map(
        per_device,
        mesh=fine,
        in_specs=placed,
        out_specs=(P(MODE, ("z",) + GROUP, None, None), P()),
        check_vma=False,
    )
```

```python
import functools
import math

import jax
import jax.numpy as jnp
from jax import lax
from jax.experimental import pallas as pl
from jax.experimental.pallas import tpu as pltpu
from jax.sharding import Mesh, PartitionSpec as P

DEGREE = 4
ROOTS = (0.0, 0.7745967, 1.0, 1.3416408)
REACH = DEGREE + 1
SUBLANES, LANES = 8, 128
UNROLL = 6

AXES = ("z", "xl", "core", "xh", "y")
GROUP = ("xl", "core")
MODE = ("xh", "y")
LAYER = ("xh", "y", "xl", "core")


def root_of(label):
    root = jnp.where(label == 1.0, ROOTS[1], 0.0)
    root = jnp.where(label == 2.0, ROOTS[2], root)
    return jnp.where(label == 3.0, ROOTS[3], root)


def inverse_root_of(label):
    value = jnp.where(label == 1.0, 1.0 / ROOTS[1], 0.0)
    value = jnp.where(label == 2.0, 1.0 / ROOTS[2], value)
    return jnp.where(label == 3.0, 1.0 / ROOTS[3], value)


def filter_kernel(bounds, lo, own, hi, out, short, share, even, odd, strong, square, degree):
    planes, height, width = degree.shape
    local = even.shape[1]
    rows = out.shape[3]
    depth = own.shape[0]
    low, high = bounds[0:1], bounds[1:2]
    centre = 0.5 * (high + low)
    scale = 1.0 / (0.5 * (high - low))
    inner = pl.ds(SUBLANES, height)
    lane = lax.broadcasted_iota(jnp.int32, (height, width), 1)

    def beside(ref, plane, *index):
        value = ref[(plane, *index, inner)]
        up = ref[(plane, *index, pl.ds(SUBLANES - 1, height))]
        down = ref[(plane, *index, pl.ds(SUBLANES + 1, height))]
        left = jnp.where(lane == 0, 0.0, pltpu.roll(value, 1, 1))
        right = jnp.where(lane == width - 1, 0.0, pltpu.roll(value, width - 1, 1))
        before, after = ref[(plane - 1, *index, inner)], ref[(plane + 1, *index, inner)]
        return value, (up + down) + (left + right) + (before + after)

    edge = jnp.zeros((SUBLANES, width), jnp.float32)

    def clear(plane, carry):
        for first in (0, SUBLANES + height):
            strong[plane, pl.ds(first, SUBLANES)] = edge
            for mode in range(local):
                even[plane, mode, pl.ds(first, SUBLANES)] = edge
                odd[plane, mode, pl.ds(first, SUBLANES)] = edge
        return carry

    lax.fori_loop(0, planes, clear, 0)

    for plane in (0, planes - 1):
        strong[plane, inner] = jnp.zeros((height, width), jnp.float32)
        for mode in range(local):
            even[plane, mode, inner] = jnp.zeros((height, width), jnp.float32)

    for source, start in ((lo, REACH - depth), (own, REACH), (hi, REACH + depth)):

        def load(index, carry, source=source, start=start):
            root = root_of(source[index, local].astype(jnp.float32))
            strong[start + index, inner] = root
            square[start + index] = root * root
            for mode in range(local):
                even[start + index, mode, inner] = root * source[index, mode].astype(jnp.float32)
            return carry

        lax.fori_loop(0, depth, load, 0, unroll=min(depth, UNROLL))

    def weigh(plane, carry):
        root, around = beside(strong, plane)
        degree[plane] = root * around
        return carry

    lax.fori_loop(1, planes - 1, weigh, 0, unroll=UNROLL)

    cur, prev = even, odd
    for step in range(DEGREE):
        factor = scale if step == 0 else 2.0 * scale

        def advance(plane, carry, cur=cur, prev=prev, factor=factor, step=step):
            here = (degree[plane] - centre) * factor
            there = square[plane] * factor
            for mode in range(local):
                value, around = beside(cur, plane, mode)
                value = here * value - there * around
                if step > 0:
                    value = value - prev[plane, mode, inner]
                prev[plane, mode, inner] = value
            return carry

        lax.fori_loop(step + 1, planes - step - 1, advance, 0, unroll=UNROLL)
        cur, prev = prev, cur

    for index in range(depth):
        plane = REACH + index
        heavy, weight = degree[plane], square[plane]
        upright = inverse_root_of(own[index, local].astype(jnp.float32))
        for mode in range(local):
            value, around = beside(cur, plane, mode)
            image = upright * (heavy * value - weight * around)
            out[:, index, mode] = (upright * value).reshape(-1, rows, width).astype(out.dtype)
            if index == 0:
                short[0, mode] = image
            elif index == depth - 1:
                short[1, mode] = image
            else:
                out[:, index, local + mode] = image.reshape(-1, rows, width).astype(out.dtype)

    for side, (outer, step) in enumerate(((REACH - depth, 1), (planes - 1 - REACH + depth, -1))):
        between = square[outer]
        for index in range(1, DEGREE):
            between = between * square[outer + step * index]
        share[side] = (8.0 * scale * scale * scale * scale) * between * strong[outer + step * DEGREE, inner]


def finish_kernel(lo, hi, far_lo, far_hi, short, share, done, out):
    out[...] = done[...]
    local = short.shape[1]
    depth, rows, width = out.shape[1], out.shape[3], out.shape[4]
    sides = ((lo, 0, far_lo, 0, 0), (hi, depth - 1, far_hi, 0, depth - 1))
    for side, (near, near_plane, far, far_plane, index) in enumerate(sides):
        weight = share[side] * root_of(far[far_plane, local].astype(jnp.float32))
        for mode in range(local):
            jump = near[near_plane, mode].astype(jnp.float32) - far[far_plane, mode].astype(jnp.float32)
            image = short[side, mode] + weight * jump
            out[:, index, local + mode] = image.reshape(-1, rows, width).astype(out.dtype)


def filtered_and_applied(bounds, far_lo, lo, own, hi, far_hi, blocks):
    depth, fields, height, width = own.shape
    local = fields - 1
    planes = depth + 2 * REACH
    rimmed = pltpu.VMEM((planes, local, height + 2 * SUBLANES, width), jnp.float32)
    root = pltpu.VMEM((planes, height + 2 * SUBLANES, width), jnp.float32)
    flat = pltpu.VMEM((planes, height, width), jnp.float32)
    vmem = pl.BlockSpec(memory_space=pltpu.VMEM)
    whole = jax.ShapeDtypeStruct((blocks, depth, 2 * local, height // blocks, width), jnp.bfloat16)
    steps = planes * local * height * width
    whole_part, short, share = pl.pallas_call(
        filter_kernel,
        out_shape=(
            whole,
            jax.ShapeDtypeStruct((2, local, height, width), jnp.float32),
            jax.ShapeDtypeStruct((2, height, width), jnp.float32),
        ),
        in_specs=[vmem] * 4,
        out_specs=(vmem,) * 3,
        scratch_shapes=[rimmed, rimmed, root, flat, flat],
        compiler_params=pltpu.CompilerParams(vmem_limit_bytes=40 * 1024 * 1024),
        cost_estimate=pl.CostEstimate(flops=100 * steps, bytes_accessed=8 * steps, transcendentals=0),
        name="chebyshev_filter",
    )(bounds, lo, own, hi)
    return pl.pallas_call(
        finish_kernel,
        out_shape=whole,
        in_specs=[vmem] * 7,
        out_specs=vmem,
        compiler_params=pltpu.CompilerParams(vmem_limit_bytes=8 * 1024 * 1024),
        name="outermost_planes",
    )(lo, hi, far_lo, far_hi, short, share, whole_part)


def pack_kernel(block, labels, out):
    group, fields = out.shape[:2]
    local = fields - 1
    tags = labels[0].astype(jnp.float32).astype(out.dtype)
    for peer in range(group):
        for mode in range(local):
            out[peer, mode] = block[peer * local + mode, 0]
        out[peer, local] = tags


def packed(block, labels, group):
    share, _, height, width = block.shape
    vmem = pl.BlockSpec(memory_space=pltpu.VMEM)
    return pl.pallas_call(
        pack_kernel,
        out_shape=jax.ShapeDtypeStruct((group, share // group + 1, height, width), block.dtype),
        in_specs=[vmem, vmem],
        out_specs=vmem,
        compiler_params=pltpu.CompilerParams(vmem_limit_bytes=8192 * 1024),
        name="pack",
    )(block, labels)


def outer_kernel(low, high, own, first, last, bounds):
    first[...] = own[: first.shape[0]]
    last[...] = own[own.shape[0] - last.shape[0] :]
    row = lax.broadcasted_iota(jnp.int32, bounds.shape, 0)
    bounds[...] = jnp.where(row == 0, low[0], high[0])


def outer_planes(filter_low, filter_high, own, extra):
    vmem, smem = pl.BlockSpec(memory_space=pltpu.VMEM), pl.BlockSpec(memory_space=pltpu.SMEM)
    plane = jax.ShapeDtypeStruct((extra,) + own.shape[1:], own.dtype)
    return pl.pallas_call(
        outer_kernel,
        out_shape=(plane, plane, jax.ShapeDtypeStruct((SUBLANES, own.shape[-1]), jnp.float32)),
        in_specs=[smem, smem, vmem],
        out_specs=(vmem,) * 3,
        compiler_params=pltpu.CompilerParams(vmem_limit_bytes=8 * 1024 * 1024),
        name="outer_planes",
    )(jnp.reshape(filter_low, (1,)), jnp.reshape(filter_high, (1,)), own)


def shifted(value, axis, step):
    size = lax.axis_size(axis)
    pairs = [(i, i + step) for i in range(size) if 0 <= i + step < size]
    return lax.ppermute(value, axis, pairs)


def summed_over_z(value):
    copies = jnp.broadcast_to(value, (lax.axis_size("z"),) + value.shape)
    return jnp.sum(lax.all_to_all(copies, "z", 0, 0, tiled=True), axis=0)


def lanes_of():
    return lax.broadcasted_iota(jnp.int32, (SUBLANES, LANES), 1)


def gram_kernel(filtered, applied, out, wide):
    size = filtered.shape[0]
    groups = size // SUBLANES
    spare = LANES - size
    full = groups - groups * spare // LANES
    lane = lanes_of()
    wide[...] = jnp.zeros(wide.shape, wide.dtype)
    contract = (((1,), (1,)), ((), ()))
    for half, source in enumerate((applied, filtered)):
        product = lax.dot_general(source[...], filtered[...], contract, preferred_element_type=jnp.float32)
        wide[half * size : (half + 1) * size, :size] = product

    def group_of(half, g):
        return wide[half * size + SUBLANES * g : half * size + SUBLANES * (g + 1), :]

    pieces = size // spare
    tiles = []
    for t in range(full):
        extra = group_of(0, full + t // pieces)
        tiles.append(jnp.where(lane < size, group_of(0, t), pltpu.roll(extra, size - spare * (t % pieces), 1)))
    for g in range(groups // 2):
        ends = SUBLANES * (g + 1)
        tiles.append(jnp.where(lane < ends, group_of(1, g), pltpu.roll(group_of(1, groups - 1 - g), ends, 1)))
    half_rows = out.shape[1]
    for t, tile in enumerate(tiles):
        out[2 * t] = tile[:half_rows]
        out[2 * t + 1] = tile[half_rows:]
    for rest in range(2 * len(tiles), out.shape[0]):
        out[rest] = jnp.zeros(out.shape[1:], out.dtype)


def packed_terms(filtered, applied, peers):
    size = filtered.shape[0]
    vmem = pl.BlockSpec(memory_space=pltpu.VMEM)
    return pl.pallas_call(
        gram_kernel,
        out_shape=jax.ShapeDtypeStruct((peers, SUBLANES // 2, LANES), jnp.float32),
        in_specs=[vmem, vmem],
        out_specs=vmem,
        scratch_shapes=[pltpu.VMEM((2 * size, LANES), jnp.float32)],
        compiler_params=pltpu.CompilerParams(vmem_limit_bytes=8 * 1024 * 1024),
        name="packed_terms",
    )(filtered, applied)


def total_over_all(partial):
    terms = lax.all_to_all(partial, LAYER, 0, 0, tiled=True)
    mine = summed_over_z(jnp.sum(terms, axis=0))
    return lax.all_to_all(jnp.broadcast_to(mine, partial.shape), LAYER, 0, 0, tiled=True)


def turn_kernel(scale, whole, filtered, inverse, crossed, turned, staged, square):
    size = inverse.shape[0]
    rows = turned.shape[2]
    groups = size // SUBLANES
    spare = LANES - size
    full = groups - groups * spare // LANES
    pieces = size // spare
    tile = (SUBLANES, LANES)
    sub = lax.broadcasted_iota(jnp.int32, tile, 0)
    lane = lanes_of()
    tiles = [jnp.concatenate([whole[2 * t], whole[2 * t + 1]], axis=0) for t in range(full + groups // 2)]

    for g in range(full):
        crossed[SUBLANES * g : SUBLANES * (g + 1), :] = tiles[g][:, :size]
    for g in range(full, groups):
        first = pieces * (g - full)
        value = pltpu.roll(tiles[first], spare, 1)
        for p in range(1, pieces):
            value = jnp.where(lane < spare * p, value, pltpu.roll(tiles[first + p], spare * (p + 1), 1))
        crossed[SUBLANES * g : SUBLANES * (g + 1), :] = value[:, :size]

    square[...] = jnp.zeros(square.shape, square.dtype)
    for g in range(groups // 2):
        ends = SUBLANES * (g + 1)
        last = groups - 1 - g
        square[SUBLANES * g : ends, :] = tiles[full + g]
        square[SUBLANES * last : SUBLANES * (last + 1), :] = pltpu.roll(tiles[full + g], LANES - ends, 1)
    mirrored = square[...].T
    left = [
        jnp.where(
            lane < SUBLANES * (g + 1),
            square[SUBLANES * g : SUBLANES * (g + 1), :],
            mirrored[SUBLANES * g : SUBLANES * (g + 1), :],
        )
        for g in range(groups)
    ]
    right = [jnp.where(lane == sub + SUBLANES * g, 1.0, 0.0) for g in range(groups)]

    def row_of(value, t):
        return jnp.broadcast_to(value[t : t + 1, :], tile)

    for b in range(groups):
        first = SUBLANES * b
        columns = [
            [jnp.broadcast_to(left[g][:, first + t : first + t + 1], tile) for g in range(b, groups)]
            for t in range(SUBLANES)
        ]
        diagonal = jnp.ones(tile, jnp.float32)
        for t in range(SUBLANES):
            pivot = row_of(columns[t][0], t)
            diagonal = jnp.where(sub == t, pivot, diagonal)
            part = 1.0 / pivot
            row_left = row_of(left[b], t) * part
            row_right = row_of(right[b], t) * part
            rest = range(t + 1, SUBLANES)
            row_columns = [row_of(columns[s][0], t) * part for s in rest]
            for g in range(b, groups):
                weight = columns[t][g - b]
                if g == b:
                    weight = jnp.where(sub > t, weight, 0.0)
                left[g] = left[g] - weight * row_left
                right[g] = right[g] - weight * row_right
                for s, row_column in zip(rest, row_columns):
                    columns[s][g - b] = columns[s][g - b] - weight * row_column
        inverse[first : first + SUBLANES, :] = (right[b] * lax.rsqrt(diagonal))[:, :size]

    rotation = inverse[...].astype(jnp.bfloat16)
    product = jnp.dot(rotation, filtered[...], preferred_element_type=jnp.float32) * scale
    width = turned.shape[3]
    for row in range(rows):
        staged[pl.ds(row, size, stride=rows), :] = product[:, row * width : (row + 1) * width]
    turned[...] = staged[...].reshape(turned.shape).astype(turned.dtype)


def inverse_and_turned(whole, filtered, scale, peers, rows):
    size = filtered.shape[0]
    width = filtered.shape[1] // rows
    vmem = pl.BlockSpec(memory_space=pltpu.VMEM)
    matrix = jax.ShapeDtypeStruct((size, size), jnp.float32)
    return pl.pallas_call(
        functools.partial(turn_kernel, scale),
        out_shape=(matrix, matrix, jax.ShapeDtypeStruct((peers, size // peers, rows, width), jnp.bfloat16)),
        in_specs=[vmem, vmem],
        out_specs=(vmem, vmem, vmem),
        scratch_shapes=[pltpu.VMEM((size * rows, width), jnp.float32), pltpu.VMEM((LANES, LANES), jnp.float32)],
        compiler_params=pltpu.CompilerParams(vmem_limit_bytes=8 * 1024 * 1024),
        name="inverse_and_turned",
    )(whole, filtered)


def projection(inverse, cross):
    return jnp.dot(
        jnp.dot(inverse, cross, precision=lax.Precision.HIGHEST),
        inverse.T,
        precision=lax.Precision.HIGHEST,
    )


def per_device(initial_block, labels, filter_low, filter_high):
    share, _, height, width = initial_block.shape
    group, blocks = lax.axis_size(GROUP), lax.axis_size(MODE)
    local = share // group
    modes = share * blocks
    rows = height // blocks
    scale = math.sqrt(height * width * group * lax.axis_size("z"))

    own = lax.all_to_all(packed(initial_block, labels, group), GROUP, 0, 0, tiled=True)
    extra = REACH - group
    lo, hi = shifted(own, "z", 1), shifted(own, "z", -1)
    first, last, bounds = outer_planes(filter_low, filter_high, own, extra)
    far_lo, far_hi = shifted(last, "z", 2), shifted(first, "z", -2)

    pair = filtered_and_applied(bounds, far_lo, lo, own, hi, far_hi, blocks)
    pair = pair.reshape(blocks * group, 2 * local, rows, width)

    pair = lax.all_to_all(pair, LAYER, 0, 0, tiled=True)
    filtered = pair[:, :local].reshape(modes, rows * width)
    applied = pair[:, local:].reshape(modes, rows * width)
    total = total_over_all(packed_terms(filtered, applied, blocks * group))
    inverse, crossed, turned = inverse_and_turned(total, filtered, scale, blocks, rows)
    projected = projection(inverse, crossed.T)
    turned = lax.all_to_all(turned, MODE, 0, 0, tiled=True)
    modes_out = jnp.transpose(turned, (1, 0, 2, 3)).reshape(share, 1, height, width)
    return (modes_out, projected)


def solution(mesh):
    devices = mesh.devices
    slabs, modes = devices.shape
    fine = Mesh(devices.reshape(slabs // 4, 2, 2, 2, modes // 2), AXES)
    placed = (P(MODE, ("z",) + GROUP, None, None), P(("z",) + GROUP, None, None), P(), P())
    return jax.shard_map(
        per_device,
        mesh=fine,
        in_specs=placed,
        out_specs=(P(MODE, ("z",) + GROUP, None, None), P()),
        check_vma=False,
    )
```

```python
import functools
import math

import jax
import jax.numpy as jnp
from jax import lax
from jax.experimental import pallas as pl
from jax.experimental.pallas import tpu as pltpu
from jax.sharding import Mesh, PartitionSpec as P

DEGREE = 4
ROOTS = (0.0, 0.7745967, 1.0, 1.3416408)
REACH = DEGREE + 1
SUBLANES, LANES = 8, 128
UNROLL = 6

AXES = ("z", "xl", "core", "xh", "y")
GROUP = ("xl", "core")
MODE = ("xh", "y")
LAYER = ("xh", "y", "xl", "core")


def root_of(label):
    root = jnp.where(label == 1.0, ROOTS[1], 0.0)
    root = jnp.where(label == 2.0, ROOTS[2], root)
    return jnp.where(label == 3.0, ROOTS[3], root)


def inverse_root_of(label):
    value = jnp.where(label == 1.0, 1.0 / ROOTS[1], 0.0)
    value = jnp.where(label == 2.0, 1.0 / ROOTS[2], value)
    return jnp.where(label == 3.0, 1.0 / ROOTS[3], value)


def filter_kernel(lowest, highest, lo, own, hi, out, short, share, even, odd, strong, square, degree):
    planes, height, width = degree.shape
    local = even.shape[1]
    rows = out.shape[3]
    depth = own.shape[0]
    low, high = lowest[0], highest[0]
    centre = 0.5 * (high + low)
    scale = 1.0 / (0.5 * (high - low))
    inner = pl.ds(SUBLANES, height)
    lane = lax.broadcasted_iota(jnp.int32, (height, width), 1)

    def beside(ref, plane, *index):
        value = ref[(plane, *index, inner)]
        up = ref[(plane, *index, pl.ds(SUBLANES - 1, height))]
        down = ref[(plane, *index, pl.ds(SUBLANES + 1, height))]
        left = jnp.where(lane == 0, 0.0, pltpu.roll(value, 1, 1))
        right = jnp.where(lane == width - 1, 0.0, pltpu.roll(value, width - 1, 1))
        before, after = ref[(plane - 1, *index, inner)], ref[(plane + 1, *index, inner)]
        return value, (up + down) + (left + right) + (before + after)

    edge = jnp.zeros((SUBLANES, width), jnp.float32)

    def clear(plane, carry):
        for first in (0, SUBLANES + height):
            strong[plane, pl.ds(first, SUBLANES)] = edge
            for mode in range(local):
                even[plane, mode, pl.ds(first, SUBLANES)] = edge
                odd[plane, mode, pl.ds(first, SUBLANES)] = edge
        return carry

    lax.fori_loop(0, planes, clear, 0)

    for plane in (0, planes - 1):
        strong[plane, inner] = jnp.zeros((height, width), jnp.float32)
        for mode in range(local):
            even[plane, mode, inner] = jnp.zeros((height, width), jnp.float32)

    for source, start in ((lo, REACH - depth), (own, REACH), (hi, REACH + depth)):

        def load(index, carry, source=source, start=start):
            root = root_of(source[index, local].astype(jnp.float32))
            strong[start + index, inner] = root
            square[start + index] = root * root
            for mode in range(local):
                even[start + index, mode, inner] = root * source[index, mode].astype(jnp.float32)
            return carry

        lax.fori_loop(0, depth, load, 0, unroll=min(depth, UNROLL))

    def weigh(plane, carry):
        root, around = beside(strong, plane)
        degree[plane] = root * around
        return carry

    lax.fori_loop(1, planes - 1, weigh, 0, unroll=UNROLL)

    cur, prev = even, odd
    for step in range(DEGREE):
        factor = scale if step == 0 else 2.0 * scale

        def advance(plane, carry, cur=cur, prev=prev, factor=factor, step=step):
            here = (degree[plane] - centre) * factor
            there = square[plane] * factor
            for mode in range(local):
                value, around = beside(cur, plane, mode)
                value = here * value - there * around
                if step > 0:
                    value = value - prev[plane, mode, inner]
                prev[plane, mode, inner] = value
            return carry

        lax.fori_loop(step + 1, planes - step - 1, advance, 0, unroll=UNROLL)
        cur, prev = prev, cur

    for index in range(depth):
        plane = REACH + index
        heavy, weight = degree[plane], square[plane]
        upright = inverse_root_of(own[index, local].astype(jnp.float32))
        for mode in range(local):
            value, around = beside(cur, plane, mode)
            image = upright * (heavy * value - weight * around)
            out[:, index, mode] = (upright * value).reshape(-1, rows, width).astype(out.dtype)
            if index == 0:
                short[0, mode] = image
            elif index == depth - 1:
                short[1, mode] = image
            else:
                out[:, index, local + mode] = image.reshape(-1, rows, width).astype(out.dtype)

    for side, (outer, step) in enumerate(((REACH - depth, 1), (planes - 1 - REACH + depth, -1))):
        between = square[outer]
        for index in range(1, DEGREE):
            between = between * square[outer + step * index]
        share[side] = (8.0 * scale * scale * scale * scale) * between * strong[outer + step * DEGREE, inner]


def finish_kernel(lo, hi, far_lo, far_hi, short, share, done, out):
    out[...] = done[...]
    local = short.shape[1]
    depth, rows, width = out.shape[1], out.shape[3], out.shape[4]
    sides = ((lo, 0, far_lo, 0, 0), (hi, depth - 1, far_hi, 0, depth - 1))
    for side, (near, near_plane, far, far_plane, index) in enumerate(sides):
        weight = share[side] * root_of(far[far_plane, local].astype(jnp.float32))
        for mode in range(local):
            jump = near[near_plane, mode].astype(jnp.float32) - far[far_plane, mode].astype(jnp.float32)
            image = short[side, mode] + weight * jump
            out[:, index, local + mode] = image.reshape(-1, rows, width).astype(out.dtype)


def filtered_and_applied(lowest, highest, far_lo, lo, own, hi, far_hi, blocks):
    depth, fields, height, width = own.shape
    local = fields - 1
    planes = depth + 2 * REACH
    rimmed = pltpu.VMEM((planes, local, height + 2 * SUBLANES, width), jnp.float32)
    root = pltpu.VMEM((planes, height + 2 * SUBLANES, width), jnp.float32)
    flat = pltpu.VMEM((planes, height, width), jnp.float32)
    vmem = pl.BlockSpec(memory_space=pltpu.VMEM)
    whole = jax.ShapeDtypeStruct((blocks, depth, 2 * local, height // blocks, width), jnp.bfloat16)
    steps = planes * local * height * width
    whole_part, short, share = pl.pallas_call(
        filter_kernel,
        out_shape=(
            whole,
            jax.ShapeDtypeStruct((2, local, height, width), jnp.float32),
            jax.ShapeDtypeStruct((2, height, width), jnp.float32),
        ),
        in_specs=[pl.BlockSpec(memory_space=pltpu.SMEM)] * 2 + [vmem] * 3,
        out_specs=(vmem,) * 3,
        scratch_shapes=[rimmed, rimmed, root, flat, flat],
        compiler_params=pltpu.CompilerParams(vmem_limit_bytes=40 * 1024 * 1024),
        cost_estimate=pl.CostEstimate(flops=100 * steps, bytes_accessed=8 * steps, transcendentals=0),
        name="chebyshev_filter",
    )(lowest, highest, lo, own, hi)
    return pl.pallas_call(
        finish_kernel,
        out_shape=whole,
        in_specs=[vmem] * 7,
        out_specs=vmem,
        compiler_params=pltpu.CompilerParams(vmem_limit_bytes=8 * 1024 * 1024),
        name="outermost_planes",
    )(lo, hi, far_lo, far_hi, short, share, whole_part)


def pack_kernel(block, labels, out):
    group, fields = out.shape[:2]
    local = fields - 1
    tags = labels[0].astype(jnp.float32).astype(out.dtype)
    for peer in range(group):
        for mode in range(local):
            out[peer, mode] = block[peer * local + mode, 0]
        out[peer, local] = tags


def packed(block, labels, group):
    share, _, height, width = block.shape
    vmem = pl.BlockSpec(memory_space=pltpu.VMEM)
    return pl.pallas_call(
        pack_kernel,
        out_shape=jax.ShapeDtypeStruct((group, share // group + 1, height, width), block.dtype),
        in_specs=[vmem, vmem],
        out_specs=vmem,
        compiler_params=pltpu.CompilerParams(vmem_limit_bytes=8 * 1024 * 1024),
        name="pack",
    )(block, labels)


def shifted(value, axis, step):
    size = lax.axis_size(axis)
    pairs = [(i, i + step) for i in range(size) if 0 <= i + step < size]
    return lax.ppermute(value, axis, pairs)


def summed_over_z(value):
    copies = jnp.broadcast_to(value, (lax.axis_size("z"),) + value.shape)
    return jnp.sum(lax.all_to_all(copies, "z", 0, 0, tiled=True), axis=0)


def lanes_of():
    return lax.broadcasted_iota(jnp.int32, (SUBLANES, LANES), 1)


def gram_kernel(filtered, applied, out, wide):
    size = filtered.shape[0]
    groups = size // SUBLANES
    spare = LANES - size
    full = groups - groups * spare // LANES
    lane = lanes_of()
    wide[...] = jnp.zeros(wide.shape, wide.dtype)
    contract = (((1,), (1,)), ((), ()))
    for half, source in enumerate((applied, filtered)):
        product = lax.dot_general(source[...], filtered[...], contract, preferred_element_type=jnp.float32)
        wide[half * size : (half + 1) * size, :size] = product

    def group_of(half, g):
        return wide[half * size + SUBLANES * g : half * size + SUBLANES * (g + 1), :]

    pieces = size // spare
    tiles = []
    for t in range(full):
        extra = group_of(0, full + t // pieces)
        tiles.append(jnp.where(lane < size, group_of(0, t), pltpu.roll(extra, size - spare * (t % pieces), 1)))
    for g in range(groups // 2):
        ends = SUBLANES * (g + 1)
        tiles.append(jnp.where(lane < ends, group_of(1, g), pltpu.roll(group_of(1, groups - 1 - g), ends, 1)))
    half_rows = out.shape[1]
    for t, tile in enumerate(tiles):
        out[2 * t] = tile[:half_rows]
        out[2 * t + 1] = tile[half_rows:]
    for rest in range(2 * len(tiles), out.shape[0]):
        out[rest] = jnp.zeros(out.shape[1:], out.dtype)


def packed_terms(filtered, applied, peers):
    size = filtered.shape[0]
    vmem = pl.BlockSpec(memory_space=pltpu.VMEM)
    return pl.pallas_call(
        gram_kernel,
        out_shape=jax.ShapeDtypeStruct((peers, SUBLANES // 2, LANES), jnp.float32),
        in_specs=[vmem, vmem],
        out_specs=vmem,
        scratch_shapes=[pltpu.VMEM((2 * size, LANES), jnp.float32)],
        compiler_params=pltpu.CompilerParams(vmem_limit_bytes=8 * 1024 * 1024),
        name="packed_terms",
    )(filtered, applied)


def total_over_all(partial):
    terms = lax.all_to_all(partial, LAYER, 0, 0, tiled=True)
    mine = summed_over_z(jnp.sum(terms, axis=0))
    return lax.all_to_all(jnp.broadcast_to(mine, partial.shape), LAYER, 0, 0, tiled=True)


def turn_kernel(scale, whole, filtered, projected, turned, inverse, crossed, result, staged, square, written):
    size = inverse.shape[0]
    rows = turned.shape[2]
    groups = size // SUBLANES
    spare = LANES - size
    full = groups - groups * spare // LANES
    pieces = size // spare
    tile = (SUBLANES, LANES)
    sub = lax.broadcasted_iota(jnp.int32, tile, 0)
    lane = lanes_of()
    tiles = [jnp.concatenate([whole[2 * t], whole[2 * t + 1]], axis=0) for t in range(full + groups // 2)]

    for g in range(full):
        crossed[SUBLANES * g : SUBLANES * (g + 1), :] = tiles[g][:, :size]
    for g in range(full, groups):
        first = pieces * (g - full)
        value = pltpu.roll(tiles[first], spare, 1)
        for p in range(1, pieces):
            value = jnp.where(lane < spare * p, value, pltpu.roll(tiles[first + p], spare * (p + 1), 1))
        crossed[SUBLANES * g : SUBLANES * (g + 1), :] = value[:, :size]

    square[...] = jnp.zeros(square.shape, square.dtype)
    for g in range(groups // 2):
        ends = SUBLANES * (g + 1)
        last = groups - 1 - g
        square[SUBLANES * g : ends, :] = tiles[full + g]
        square[SUBLANES * last : SUBLANES * (last + 1), :] = pltpu.roll(tiles[full + g], LANES - ends, 1)
    mirrored = square[...].T
    left = [
        jnp.where(
            lane < SUBLANES * (g + 1),
            square[SUBLANES * g : SUBLANES * (g + 1), :],
            mirrored[SUBLANES * g : SUBLANES * (g + 1), :],
        )
        for g in range(groups)
    ]
    right = [jnp.where(lane == sub + SUBLANES * g, 1.0, 0.0) for g in range(groups)]

    def row_of(value, t):
        return jnp.broadcast_to(value[t : t + 1, :], tile)

    for b in range(groups):
        first = SUBLANES * b
        columns = [
            [jnp.broadcast_to(left[g][:, first + t : first + t + 1], tile) for g in range(b, groups)]
            for t in range(SUBLANES)
        ]
        diagonal = jnp.ones(tile, jnp.float32)
        for t in range(SUBLANES):
            pivot = row_of(columns[t][0], t)
            diagonal = jnp.where(sub == t, pivot, diagonal)
            part = 1.0 / pivot
            row_left = row_of(left[b], t) * part
            row_right = row_of(right[b], t) * part
            rest = range(t + 1, SUBLANES)
            row_columns = [row_of(columns[s][0], t) * part for s in rest]
            for g in range(b, groups):
                weight = columns[t][g - b]
                if g == b:
                    weight = jnp.where(sub > t, weight, 0.0)
                left[g] = left[g] - weight * row_left
                right[g] = right[g] - weight * row_right
                for s, row_column in zip(rest, row_columns):
                    columns[s][g - b] = columns[s][g - b] - weight * row_column
        inverse[first : first + SUBLANES, :] = (right[b] * lax.rsqrt(diagonal))[:, :size]

    contract = (((1,), (1,)), ((), ()))
    exact = dict(precision=lax.Precision.HIGHEST, preferred_element_type=jnp.float32)
    half = lax.dot_general(inverse[...], crossed[...], contract, **exact)
    result[...] = lax.dot_general(half, inverse[...], contract, **exact)
    write = pltpu.make_async_copy(result, projected, written)
    write.start()

    rotation = inverse[...].astype(jnp.bfloat16)
    product = jnp.dot(rotation, filtered[...], preferred_element_type=jnp.float32) * scale
    width = turned.shape[3]
    for row in range(rows):
        staged[pl.ds(row, size, stride=rows), :] = product[:, row * width : (row + 1) * width]
    turned[...] = staged[...].reshape(turned.shape).astype(turned.dtype)
    write.wait()


def projected_and_turned(whole, filtered, scale, peers, rows):
    size = filtered.shape[0]
    width = filtered.shape[1] // rows
    vmem = pl.BlockSpec(memory_space=pltpu.VMEM)
    matrix = pltpu.VMEM((size, size), jnp.float32)
    return pl.pallas_call(
        functools.partial(turn_kernel, scale),
        out_shape=(
            jax.ShapeDtypeStruct((size, size), jnp.float32),
            jax.ShapeDtypeStruct((peers, size // peers, rows, width), jnp.bfloat16),
        ),
        in_specs=[vmem, vmem],
        out_specs=(pl.BlockSpec(memory_space=pl.ANY), vmem),
        scratch_shapes=[
            matrix,
            matrix,
            matrix,
            pltpu.VMEM((size * rows, width), jnp.float32),
            pltpu.VMEM((LANES, LANES), jnp.float32),
            pltpu.SemaphoreType.DMA,
        ],
        compiler_params=pltpu.CompilerParams(vmem_limit_bytes=8 * 1024 * 1024),
        name="projected_and_turned",
    )(whole, filtered)


def per_device(initial_block, labels, filter_low, filter_high):
    share, _, height, width = initial_block.shape
    group, blocks = lax.axis_size(GROUP), lax.axis_size(MODE)
    local = share // group
    modes = share * blocks
    rows = height // blocks
    scale = math.sqrt(height * width * group * lax.axis_size("z"))

    own = lax.all_to_all(packed(initial_block, labels, group), GROUP, 0, 0, tiled=True)
    extra = REACH - group
    lo, hi = shifted(own, "z", 1), shifted(own, "z", -1)
    far_lo, far_hi = shifted(own[group - extra :], "z", 2), shifted(own[:extra], "z", -2)

    lowest, highest = jnp.reshape(filter_low, (1,)), jnp.reshape(filter_high, (1,))
    pair = filtered_and_applied(lowest, highest, far_lo, lo, own, hi, far_hi, blocks)
    pair = pair.reshape(blocks * group, 2 * local, rows, width)

    pair = lax.all_to_all(pair, LAYER, 0, 0, tiled=True)
    filtered = pair[:, :local].reshape(modes, rows * width)
    applied = pair[:, local:].reshape(modes, rows * width)
    total = total_over_all(packed_terms(filtered, applied, blocks * group))
    projected, turned = projected_and_turned(total, filtered, scale, blocks, rows)
    turned = lax.all_to_all(turned, MODE, 0, 0, tiled=True)
    modes_out = jnp.transpose(turned, (1, 0, 2, 3)).reshape(share, 1, height, width)
    return (modes_out, projected)


def solution(mesh):
    devices = mesh.devices
    slabs, modes = devices.shape
    fine = Mesh(devices.reshape(slabs // 4, 2, 2, 2, modes // 2), AXES)
    placed = (P(MODE, ("z",) + GROUP, None, None), P(("z",) + GROUP, None, None), P(), P())
    return jax.shard_map(
        per_device,
        mesh=fine,
        in_specs=placed,
        out_specs=(P(MODE, ("z",) + GROUP, None, None), P()),
        check_vma=False,
    )
```

```python
import functools
import math

import jax
import jax.numpy as jnp
from jax import lax
from jax.experimental import pallas as pl
from jax.experimental.pallas import tpu as pltpu
from jax.sharding import Mesh, PartitionSpec as P

DEGREE = 4
ROOTS = (0.0, 0.7745967, 1.0, 1.3416408)
REACH = DEGREE + 1
SUBLANES, LANES = 8, 128
UNROLL = 6

AXES = ("z", "xl", "core", "xh", "y")
GROUP = ("xl", "core")
MODE = ("xh", "y")
LAYER = ("xh", "y", "xl", "core")


def root_of(label):
    root = jnp.where(label == 1.0, ROOTS[1], 0.0)
    root = jnp.where(label == 2.0, ROOTS[2], root)
    return jnp.where(label == 3.0, ROOTS[3], root)


def inverse_root_of(label):
    value = jnp.where(label == 1.0, 1.0 / ROOTS[1], 0.0)
    value = jnp.where(label == 2.0, 1.0 / ROOTS[2], value)
    return jnp.where(label == 3.0, 1.0 / ROOTS[3], value)


def filter_kernel(lowest, highest, lo, own, hi, out, short, share, even, odd, strong, square, degree):
    planes, height, width = degree.shape
    local = even.shape[1]
    rows = out.shape[3]
    depth = own.shape[0]
    low, high = lowest[...], highest[...]
    centre = 0.5 * (high + low)
    scale = 1.0 / (0.5 * (high - low))
    inner = pl.ds(SUBLANES, height)
    lane = lax.broadcasted_iota(jnp.int32, (height, width), 1)

    def beside(ref, plane, *index):
        value = ref[(plane, *index, inner)]
        up = ref[(plane, *index, pl.ds(SUBLANES - 1, height))]
        down = ref[(plane, *index, pl.ds(SUBLANES + 1, height))]
        left = jnp.where(lane == 0, 0.0, pltpu.roll(value, 1, 1))
        right = jnp.where(lane == width - 1, 0.0, pltpu.roll(value, width - 1, 1))
        before, after = ref[(plane - 1, *index, inner)], ref[(plane + 1, *index, inner)]
        return value, (up + down) + (left + right) + (before + after)

    edge = jnp.zeros((SUBLANES, width), jnp.float32)

    def clear(plane, carry):
        for first in (0, SUBLANES + height):
            strong[plane, pl.ds(first, SUBLANES)] = edge
            for mode in range(local):
                even[plane, mode, pl.ds(first, SUBLANES)] = edge
                odd[plane, mode, pl.ds(first, SUBLANES)] = edge
        return carry

    lax.fori_loop(0, planes, clear, 0)

    for plane in (0, planes - 1):
        strong[plane, inner] = jnp.zeros((height, width), jnp.float32)
        for mode in range(local):
            even[plane, mode, inner] = jnp.zeros((height, width), jnp.float32)

    for source, start in ((lo, REACH - depth), (own, REACH), (hi, REACH + depth)):

        def load(index, carry, source=source, start=start):
            root = root_of(source[index, local].astype(jnp.float32))
            strong[start + index, inner] = root
            square[start + index] = root * root
            for mode in range(local):
                even[start + index, mode, inner] = root * source[index, mode].astype(jnp.float32)
            return carry

        lax.fori_loop(0, depth, load, 0, unroll=min(depth, UNROLL))

    def weigh(plane, carry):
        root, around = beside(strong, plane)
        degree[plane] = root * around
        return carry

    lax.fori_loop(1, planes - 1, weigh, 0, unroll=UNROLL)

    cur, prev = even, odd
    for step in range(DEGREE):
        factor = scale if step == 0 else 2.0 * scale

        def advance(plane, carry, cur=cur, prev=prev, factor=factor, step=step):
            here = (degree[plane] - centre) * factor
            there = square[plane] * factor
            for mode in range(local):
                value, around = beside(cur, plane, mode)
                value = here * value - there * around
                if step > 0:
                    value = value - prev[plane, mode, inner]
                prev[plane, mode, inner] = value
            return carry

        lax.fori_loop(step + 1, planes - step - 1, advance, 0, unroll=UNROLL)
        cur, prev = prev, cur

    for index in range(depth):
        plane = REACH + index
        heavy, weight = degree[plane], square[plane]
        upright = inverse_root_of(own[index, local].astype(jnp.float32))
        for mode in range(local):
            value, around = beside(cur, plane, mode)
            image = upright * (heavy * value - weight * around)
            out[:, index, mode] = (upright * value).reshape(-1, rows, width).astype(out.dtype)
            if index == 0:
                short[0, mode] = image
            elif index == depth - 1:
                short[1, mode] = image
            else:
                out[:, index, local + mode] = image.reshape(-1, rows, width).astype(out.dtype)

    for side, (outer, step) in enumerate(((REACH - depth, 1), (planes - 1 - REACH + depth, -1))):
        between = square[outer]
        for index in range(1, DEGREE):
            between = between * square[outer + step * index]
        share[side] = (8.0 * scale * scale * scale * scale) * between * strong[outer + step * DEGREE, inner]


def finish_kernel(lo, hi, far_lo, far_hi, short, share, done, out):
    out[...] = done[...]
    local = short.shape[1]
    depth, rows, width = out.shape[1], out.shape[3], out.shape[4]
    sides = ((lo, 0, far_lo, 0, 0), (hi, depth - 1, far_hi, 0, depth - 1))
    for side, (near, near_plane, far, far_plane, index) in enumerate(sides):
        weight = share[side] * root_of(far[far_plane, local].astype(jnp.float32))
        for mode in range(local):
            jump = near[near_plane, mode].astype(jnp.float32) - far[far_plane, mode].astype(jnp.float32)
            image = short[side, mode] + weight * jump
            out[:, index, local + mode] = image.reshape(-1, rows, width).astype(out.dtype)


def filtered_and_applied(lowest, highest, far_lo, lo, own, hi, far_hi, blocks):
    depth, fields, height, width = own.shape
    local = fields - 1
    planes = depth + 2 * REACH
    rimmed = pltpu.VMEM((planes, local, height + 2 * SUBLANES, width), jnp.float32)
    root = pltpu.VMEM((planes, height + 2 * SUBLANES, width), jnp.float32)
    flat = pltpu.VMEM((planes, height, width), jnp.float32)
    vmem = pl.BlockSpec(memory_space=pltpu.VMEM)
    whole = jax.ShapeDtypeStruct((blocks, depth, 2 * local, height // blocks, width), jnp.bfloat16)
    steps = planes * local * height * width
    whole_part, short, share = pl.pallas_call(
        filter_kernel,
        out_shape=(
            whole,
            jax.ShapeDtypeStruct((2, local, height, width), jnp.float32),
            jax.ShapeDtypeStruct((2, height, width), jnp.float32),
        ),
        in_specs=[pl.BlockSpec(memory_space=pltpu.SMEM)] * 2 + [vmem] * 3,
        out_specs=(vmem,) * 3,
        scratch_shapes=[rimmed, rimmed, root, flat, flat],
        compiler_params=pltpu.CompilerParams(vmem_limit_bytes=40 * 1024 * 1024),
        cost_estimate=pl.CostEstimate(flops=100 * steps, bytes_accessed=8 * steps, transcendentals=0),
        name="chebyshev_filter",
    )(lowest, highest, lo, own, hi)
    return pl.pallas_call(
        finish_kernel,
        out_shape=whole,
        in_specs=[vmem] * 7,
        out_specs=vmem,
        compiler_params=pltpu.CompilerParams(vmem_limit_bytes=8 * 1024 * 1024),
        name="outermost_planes",
    )(lo, hi, far_lo, far_hi, short, share, whole_part)


def pack_kernel(block, labels, out):
    group, fields = out.shape[:2]
    local = fields - 1
    tags = labels[0].astype(jnp.float32).astype(out.dtype)
    for peer in range(group):
        for mode in range(local):
            out[peer, mode] = block[peer * local + mode, 0]
        out[peer, local] = tags


def packed(block, labels, group):
    share, _, height, width = block.shape
    vmem = pl.BlockSpec(memory_space=pltpu.VMEM)
    return pl.pallas_call(
        pack_kernel,
        out_shape=jax.ShapeDtypeStruct((group, share // group + 1, height, width), block.dtype),
        in_specs=[vmem, vmem],
        out_specs=vmem,
        compiler_params=pltpu.CompilerParams(vmem_limit_bytes=8 * 1024 * 1024),
        name="pack",
    )(block, labels)


def shifted(value, axis, step):
    size = lax.axis_size(axis)
    pairs = [(i, i + step) for i in range(size) if 0 <= i + step < size]
    return lax.ppermute(value, axis, pairs)


def summed_over_z(value):
    copies = jnp.broadcast_to(value, (lax.axis_size("z"),) + value.shape)
    return jnp.sum(lax.all_to_all(copies, "z", 0, 0, tiled=True), axis=0)


def lanes_of():
    return lax.broadcasted_iota(jnp.int32, (SUBLANES, LANES), 1)


def gram_kernel(filtered, applied, out, wide):
    size = filtered.shape[0]
    groups = size // SUBLANES
    spare = LANES - size
    full = groups - groups * spare // LANES
    lane = lanes_of()
    wide[...] = jnp.zeros(wide.shape, wide.dtype)
    contract = (((1,), (1,)), ((), ()))
    for half, source in enumerate((applied, filtered)):
        product = lax.dot_general(source[...], filtered[...], contract, preferred_element_type=jnp.float32)
        wide[half * size : (half + 1) * size, :size] = product

    def group_of(half, g):
        return wide[half * size + SUBLANES * g : half * size + SUBLANES * (g + 1), :]

    pieces = size // spare
    tiles = []
    for t in range(full):
        extra = group_of(0, full + t // pieces)
        tiles.append(jnp.where(lane < size, group_of(0, t), pltpu.roll(extra, size - spare * (t % pieces), 1)))
    for g in range(groups // 2):
        ends = SUBLANES * (g + 1)
        tiles.append(jnp.where(lane < ends, group_of(1, g), pltpu.roll(group_of(1, groups - 1 - g), ends, 1)))
    half_rows = out.shape[1]
    for t, tile in enumerate(tiles):
        out[2 * t] = tile[:half_rows]
        out[2 * t + 1] = tile[half_rows:]
    for rest in range(2 * len(tiles), out.shape[0]):
        out[rest] = jnp.zeros(out.shape[1:], out.dtype)


def packed_terms(filtered, applied, peers):
    size = filtered.shape[0]
    vmem = pl.BlockSpec(memory_space=pltpu.VMEM)
    return pl.pallas_call(
        gram_kernel,
        out_shape=jax.ShapeDtypeStruct((peers, SUBLANES // 2, LANES), jnp.float32),
        in_specs=[vmem, vmem],
        out_specs=vmem,
        scratch_shapes=[pltpu.VMEM((2 * size, LANES), jnp.float32)],
        compiler_params=pltpu.CompilerParams(vmem_limit_bytes=8 * 1024 * 1024),
        name="packed_terms",
    )(filtered, applied)


def total_over_all(partial):
    terms = lax.all_to_all(partial, LAYER, 0, 0, tiled=True)
    mine = summed_over_z(jnp.sum(terms, axis=0))
    return lax.all_to_all(jnp.broadcast_to(mine, partial.shape), LAYER, 0, 0, tiled=True)


def turn_kernel(scale, whole, filtered, projected, turned, inverse, crossed, result, staged, square, written):
    size = inverse.shape[0]
    rows = turned.shape[2]
    groups = size // SUBLANES
    spare = LANES - size
    full = groups - groups * spare // LANES
    pieces = size // spare
    tile = (SUBLANES, LANES)
    sub = lax.broadcasted_iota(jnp.int32, tile, 0)
    lane = lanes_of()
    tiles = [jnp.concatenate([whole[2 * t], whole[2 * t + 1]], axis=0) for t in range(full + groups // 2)]

    for g in range(full):
        crossed[SUBLANES * g : SUBLANES * (g + 1), :] = tiles[g][:, :size]
    for g in range(full, groups):
        first = pieces * (g - full)
        value = pltpu.roll(tiles[first], spare, 1)
        for p in range(1, pieces):
            value = jnp.where(lane < spare * p, value, pltpu.roll(tiles[first + p], spare * (p + 1), 1))
        crossed[SUBLANES * g : SUBLANES * (g + 1), :] = value[:, :size]

    square[...] = jnp.zeros(square.shape, square.dtype)
    for g in range(groups // 2):
        ends = SUBLANES * (g + 1)
        last = groups - 1 - g
        square[SUBLANES * g : ends, :] = tiles[full + g]
        square[SUBLANES * last : SUBLANES * (last + 1), :] = pltpu.roll(tiles[full + g], LANES - ends, 1)
    mirrored = square[...].T
    left = [
        jnp.where(
            lane < SUBLANES * (g + 1),
            square[SUBLANES * g : SUBLANES * (g + 1), :],
            mirrored[SUBLANES * g : SUBLANES * (g + 1), :],
        )
        for g in range(groups)
    ]
    right = [jnp.where(lane == sub + SUBLANES * g, 1.0, 0.0) for g in range(groups)]

    def row_of(value, t):
        return jnp.broadcast_to(value[t : t + 1, :], tile)

    for b in range(groups):
        first = SUBLANES * b
        columns = [
            [jnp.broadcast_to(left[g][:, first + t : first + t + 1], tile) for g in range(b, groups)]
            for t in range(SUBLANES)
        ]
        diagonal = jnp.ones(tile, jnp.float32)
        for t in range(SUBLANES):
            pivot = row_of(columns[t][0], t)
            diagonal = jnp.where(sub == t, pivot, diagonal)
            part = 1.0 / pivot
            row_left = row_of(left[b], t) * part
            row_right = row_of(right[b], t) * part
            rest = range(t + 1, SUBLANES)
            row_columns = [row_of(columns[s][0], t) * part for s in rest]
            for g in range(b, groups):
                weight = columns[t][g - b]
                if g == b:
                    weight = jnp.where(sub > t, weight, 0.0)
                left[g] = left[g] - weight * row_left
                right[g] = right[g] - weight * row_right
                for s, row_column in zip(rest, row_columns):
                    columns[s][g - b] = columns[s][g - b] - weight * row_column
        inverse[first : first + SUBLANES, :] = (right[b] * lax.rsqrt(diagonal))[:, :size]

    contract = (((1,), (1,)), ((), ()))
    exact = dict(precision=lax.Precision.HIGHEST, preferred_element_type=jnp.float32)
    half = lax.dot_general(inverse[...], crossed[...], contract, **exact)
    result[...] = lax.dot_general(half, inverse[...], contract, **exact)
    write = pltpu.make_async_copy(result, projected, written)
    write.start()

    rotation = inverse[...].astype(jnp.bfloat16)
    product = jnp.dot(rotation, filtered[...], preferred_element_type=jnp.float32) * scale
    width = turned.shape[3]
    for row in range(rows):
        staged[pl.ds(row, size, stride=rows), :] = product[:, row * width : (row + 1) * width]
    turned[...] = staged[...].reshape(turned.shape).astype(turned.dtype)
    write.wait()


def projected_and_turned(whole, filtered, scale, peers, rows):
    size = filtered.shape[0]
    width = filtered.shape[1] // rows
    vmem = pl.BlockSpec(memory_space=pltpu.VMEM)
    matrix = pltpu.VMEM((size, size), jnp.float32)
    return pl.pallas_call(
        functools.partial(turn_kernel, scale),
        out_shape=(
            jax.ShapeDtypeStruct((size, size), jnp.float32),
            jax.ShapeDtypeStruct((peers, size // peers, rows, width), jnp.bfloat16),
        ),
        in_specs=[vmem, vmem],
        out_specs=(pl.BlockSpec(memory_space=pl.ANY), vmem),
        scratch_shapes=[
            matrix,
            matrix,
            matrix,
            pltpu.VMEM((size * rows, width), jnp.float32),
            pltpu.VMEM((LANES, LANES), jnp.float32),
            pltpu.SemaphoreType.DMA,
        ],
        compiler_params=pltpu.CompilerParams(vmem_limit_bytes=8 * 1024 * 1024),
        name="projected_and_turned",
    )(whole, filtered)


def per_device(initial_block, labels, filter_low, filter_high):
    share, _, height, width = initial_block.shape
    group, blocks = lax.axis_size(GROUP), lax.axis_size(MODE)
    local = share // group
    modes = share * blocks
    rows = height // blocks
    scale = math.sqrt(height * width * group * lax.axis_size("z"))

    own = lax.all_to_all(packed(initial_block, labels, group), GROUP, 0, 0, tiled=True)
    extra = REACH - group
    lo, hi = shifted(own, "z", 1), shifted(own, "z", -1)
    far_lo, far_hi = shifted(own[group - extra :], "z", 2), shifted(own[:extra], "z", -2)

    lowest, highest = filter_low, filter_high
    pair = filtered_and_applied(lowest, highest, far_lo, lo, own, hi, far_hi, blocks)
    pair = pair.reshape(blocks * group, 2 * local, rows, width)

    pair = lax.all_to_all(pair, LAYER, 0, 0, tiled=True)
    filtered = pair[:, :local].reshape(modes, rows * width)
    applied = pair[:, local:].reshape(modes, rows * width)
    total = total_over_all(packed_terms(filtered, applied, blocks * group))
    projected, turned = projected_and_turned(total, filtered, scale, blocks, rows)
    turned = lax.all_to_all(turned, MODE, 0, 0, tiled=True)
    modes_out = jnp.transpose(turned, (1, 0, 2, 3)).reshape(share, 1, height, width)
    return (modes_out, projected)


def solution(mesh):
    devices = mesh.devices
    slabs, modes = devices.shape
    fine = Mesh(devices.reshape(slabs // 4, 2, 2, 2, modes // 2), AXES)
    placed = (P(MODE, ("z",) + GROUP, None, None), P(("z",) + GROUP, None, None), P(), P())
    return jax.shard_map(
        per_device,
        mesh=fine,
        in_specs=placed,
        out_specs=(P(MODE, ("z",) + GROUP, None, None), P()),
        check_vma=False,
    )
```

```python
import functools
import math

import jax
import jax.numpy as jnp
from jax import lax
from jax.experimental import pallas as pl
from jax.experimental.pallas import tpu as pltpu
from jax.sharding import Mesh, PartitionSpec as P

DEGREE = 4
ROOTS = (0.0, 0.7745967, 1.0, 1.3416408)
REACH = DEGREE + 1
SUBLANES, LANES = 8, 128
UNROLL = 6

AXES = ("z", "xl", "core", "xh", "y")
GROUP = ("xl", "core")
MODE = ("xh", "y")
LAYER = ("xh", "y", "xl", "core")


def root_of(label):
    root = jnp.where(label == 1.0, ROOTS[1], 0.0)
    root = jnp.where(label == 2.0, ROOTS[2], root)
    return jnp.where(label == 3.0, ROOTS[3], root)


def inverse_root_of(label):
    value = jnp.where(label == 1.0, 1.0 / ROOTS[1], 0.0)
    value = jnp.where(label == 2.0, 1.0 / ROOTS[2], value)
    return jnp.where(label == 3.0, 1.0 / ROOTS[3], value)


def filter_kernel(lowest, highest, lo, own, hi, out, short, share, even, odd, strong, square, degree):
    planes, height, width = degree.shape
    local = even.shape[1]
    rows = out.shape[3]
    depth = own.shape[0]
    low, high = lowest[...], highest[...]
    centre = 0.5 * (high + low)
    scale = 1.0 / (0.5 * (high - low))
    inner = pl.ds(SUBLANES, height)
    lane = lax.broadcasted_iota(jnp.int32, (height, width), 1)

    def beside(ref, plane, *index):
        value = ref[(plane, *index, inner)]
        up = ref[(plane, *index, pl.ds(SUBLANES - 1, height))]
        down = ref[(plane, *index, pl.ds(SUBLANES + 1, height))]
        left = jnp.where(lane == 0, 0.0, pltpu.roll(value, 1, 1))
        right = jnp.where(lane == width - 1, 0.0, pltpu.roll(value, width - 1, 1))
        before, after = ref[(plane - 1, *index, inner)], ref[(plane + 1, *index, inner)]
        return value, (up + down) + (left + right) + (before + after)

    edge = jnp.zeros((SUBLANES, width), jnp.float32)

    def clear(plane, carry):
        for first in (0, SUBLANES + height):
            strong[plane, pl.ds(first, SUBLANES)] = edge
            for mode in range(local):
                even[plane, mode, pl.ds(first, SUBLANES)] = edge
                odd[plane, mode, pl.ds(first, SUBLANES)] = edge
        return carry

    lax.fori_loop(0, planes, clear, 0, unroll=planes // 2)

    for plane in (0, planes - 1):
        strong[plane, inner] = jnp.zeros((height, width), jnp.float32)
        for mode in range(local):
            even[plane, mode, inner] = jnp.zeros((height, width), jnp.float32)

    for source, start in ((lo, REACH - depth), (own, REACH), (hi, REACH + depth)):

        def load(index, carry, source=source, start=start):
            root = root_of(source[index, local].astype(jnp.float32))
            strong[start + index, inner] = root
            square[start + index] = root * root
            for mode in range(local):
                even[start + index, mode, inner] = root * source[index, mode].astype(jnp.float32)
            return carry

        lax.fori_loop(0, depth, load, 0, unroll=min(depth, UNROLL))

    def weigh(plane, carry):
        root, around = beside(strong, plane)
        degree[plane] = root * around
        return carry

    lax.fori_loop(1, planes - 1, weigh, 0, unroll=UNROLL)

    cur, prev = even, odd
    for step in range(DEGREE):
        factor = scale if step == 0 else 2.0 * scale

        def advance(plane, carry, cur=cur, prev=prev, factor=factor, step=step):
            here = (degree[plane] - centre) * factor
            there = square[plane] * factor
            for mode in range(local):
                value, around = beside(cur, plane, mode)
                value = here * value - there * around
                if step > 0:
                    value = value - prev[plane, mode, inner]
                prev[plane, mode, inner] = value
            return carry

        lax.fori_loop(step + 1, planes - step - 1, advance, 0, unroll=UNROLL)
        cur, prev = prev, cur

    for index in range(depth):
        plane = REACH + index
        heavy, weight = degree[plane], square[plane]
        upright = inverse_root_of(own[index, local].astype(jnp.float32))
        for mode in range(local):
            value, around = beside(cur, plane, mode)
            image = upright * (heavy * value - weight * around)
            out[:, index, mode] = (upright * value).reshape(-1, rows, width).astype(out.dtype)
            if index == 0:
                short[0, mode] = image
            elif index == depth - 1:
                short[1, mode] = image
            else:
                out[:, index, local + mode] = image.reshape(-1, rows, width).astype(out.dtype)

    for side, (outer, step) in enumerate(((REACH - depth, 1), (planes - 1 - REACH + depth, -1))):
        between = square[outer]
        for index in range(1, DEGREE):
            between = between * square[outer + step * index]
        share[side] = (8.0 * scale * scale * scale * scale) * between * strong[outer + step * DEGREE, inner]


def finish_kernel(lo, hi, far_lo, far_hi, short, share, done, out):
    out[...] = done[...]
    local = short.shape[1]
    depth, rows, width = out.shape[1], out.shape[3], out.shape[4]
    sides = ((lo, 0, far_lo, 0, 0), (hi, depth - 1, far_hi, 0, depth - 1))
    for side, (near, near_plane, far, far_plane, index) in enumerate(sides):
        weight = share[side] * root_of(far[far_plane, local].astype(jnp.float32))
        for mode in range(local):
            jump = near[near_plane, mode].astype(jnp.float32) - far[far_plane, mode].astype(jnp.float32)
            image = short[side, mode] + weight * jump
            out[:, index, local + mode] = image.reshape(-1, rows, width).astype(out.dtype)


def filtered_and_applied(lowest, highest, far_lo, lo, own, hi, far_hi, blocks):
    depth, fields, height, width = own.shape
    local = fields - 1
    planes = depth + 2 * REACH
    rimmed = pltpu.VMEM((planes, local, height + 2 * SUBLANES, width), jnp.float32)
    root = pltpu.VMEM((planes, height + 2 * SUBLANES, width), jnp.float32)
    flat = pltpu.VMEM((planes, height, width), jnp.float32)
    vmem = pl.BlockSpec(memory_space=pltpu.VMEM)
    whole = jax.ShapeDtypeStruct((blocks, depth, 2 * local, height // blocks, width), jnp.bfloat16)
    steps = planes * local * height * width
    whole_part, short, share = pl.pallas_call(
        filter_kernel,
        out_shape=(
            whole,
            jax.ShapeDtypeStruct((2, local, height, width), jnp.float32),
            jax.ShapeDtypeStruct((2, height, width), jnp.float32),
        ),
        in_specs=[pl.BlockSpec(memory_space=pltpu.SMEM)] * 2 + [vmem] * 3,
        out_specs=(vmem,) * 3,
        scratch_shapes=[rimmed, rimmed, root, flat, flat],
        compiler_params=pltpu.CompilerParams(vmem_limit_bytes=40 * 1024 * 1024),
        cost_estimate=pl.CostEstimate(flops=100 * steps, bytes_accessed=8 * steps, transcendentals=0),
        name="chebyshev_filter",
    )(lowest, highest, lo, own, hi)
    return pl.pallas_call(
        finish_kernel,
        out_shape=whole,
        in_specs=[vmem] * 7,
        out_specs=vmem,
        compiler_params=pltpu.CompilerParams(vmem_limit_bytes=8 * 1024 * 1024),
        name="outermost_planes",
    )(lo, hi, far_lo, far_hi, short, share, whole_part)


def pack_kernel(block, labels, out):
    group, fields = out.shape[:2]
    local = fields - 1
    tags = labels[0].astype(jnp.float32).astype(out.dtype)
    for peer in range(group):
        for mode in range(local):
            out[peer, mode] = block[peer * local + mode, 0]
        out[peer, local] = tags


def packed(block, labels, group):
    share, _, height, width = block.shape
    vmem = pl.BlockSpec(memory_space=pltpu.VMEM)
    return pl.pallas_call(
        pack_kernel,
        out_shape=jax.ShapeDtypeStruct((group, share // group + 1, height, width), block.dtype),
        in_specs=[vmem, vmem],
        out_specs=vmem,
        compiler_params=pltpu.CompilerParams(vmem_limit_bytes=8 * 1024 * 1024),
        name="pack",
    )(block, labels)


def shifted(value, axis, step):
    size = lax.axis_size(axis)
    pairs = [(i, i + step) for i in range(size) if 0 <= i + step < size]
    return lax.ppermute(value, axis, pairs)


def summed_over_z(value):
    copies = jnp.broadcast_to(value, (lax.axis_size("z"),) + value.shape)
    return jnp.sum(lax.all_to_all(copies, "z", 0, 0, tiled=True), axis=0)


def lanes_of():
    return lax.broadcasted_iota(jnp.int32, (SUBLANES, LANES), 1)


def gram_kernel(filtered, applied, out, wide):
    size = filtered.shape[0]
    groups = size // SUBLANES
    spare = LANES - size
    full = groups - groups * spare // LANES
    lane = lanes_of()
    wide[...] = jnp.zeros(wide.shape, wide.dtype)
    contract = (((1,), (1,)), ((), ()))
    for half, source in enumerate((applied, filtered)):
        product = lax.dot_general(source[...], filtered[...], contract, preferred_element_type=jnp.float32)
        wide[half * size : (half + 1) * size, :size] = product

    def group_of(half, g):
        return wide[half * size + SUBLANES * g : half * size + SUBLANES * (g + 1), :]

    pieces = size // spare
    tiles = []
    for t in range(full):
        extra = group_of(0, full + t // pieces)
        tiles.append(jnp.where(lane < size, group_of(0, t), pltpu.roll(extra, size - spare * (t % pieces), 1)))
    for g in range(groups // 2):
        ends = SUBLANES * (g + 1)
        tiles.append(jnp.where(lane < ends, group_of(1, g), pltpu.roll(group_of(1, groups - 1 - g), ends, 1)))
    half_rows = out.shape[1]
    for t, tile in enumerate(tiles):
        out[2 * t] = tile[:half_rows]
        out[2 * t + 1] = tile[half_rows:]
    for rest in range(2 * len(tiles), out.shape[0]):
        out[rest] = jnp.zeros(out.shape[1:], out.dtype)


def packed_terms(filtered, applied, peers):
    size = filtered.shape[0]
    vmem = pl.BlockSpec(memory_space=pltpu.VMEM)
    return pl.pallas_call(
        gram_kernel,
        out_shape=jax.ShapeDtypeStruct((peers, SUBLANES // 2, LANES), jnp.float32),
        in_specs=[vmem, vmem],
        out_specs=vmem,
        scratch_shapes=[pltpu.VMEM((2 * size, LANES), jnp.float32)],
        compiler_params=pltpu.CompilerParams(vmem_limit_bytes=8 * 1024 * 1024),
        name="packed_terms",
    )(filtered, applied)


def total_over_all(partial):
    terms = lax.all_to_all(partial, LAYER, 0, 0, tiled=True)
    mine = summed_over_z(jnp.sum(terms, axis=0))
    return lax.all_to_all(jnp.broadcast_to(mine, partial.shape), LAYER, 0, 0, tiled=True)


def turn_kernel(scale, whole, filtered, projected, turned, inverse, crossed, result, staged, square, written):
    size = inverse.shape[0]
    rows = turned.shape[2]
    groups = size // SUBLANES
    spare = LANES - size
    full = groups - groups * spare // LANES
    pieces = size // spare
    tile = (SUBLANES, LANES)
    sub = lax.broadcasted_iota(jnp.int32, tile, 0)
    lane = lanes_of()
    tiles = [jnp.concatenate([whole[2 * t], whole[2 * t + 1]], axis=0) for t in range(full + groups // 2)]

    for g in range(full):
        crossed[SUBLANES * g : SUBLANES * (g + 1), :] = tiles[g][:, :size]
    for g in range(full, groups):
        first = pieces * (g - full)
        value = pltpu.roll(tiles[first], spare, 1)
        for p in range(1, pieces):
            value = jnp.where(lane < spare * p, value, pltpu.roll(tiles[first + p], spare * (p + 1), 1))
        crossed[SUBLANES * g : SUBLANES * (g + 1), :] = value[:, :size]

    square[...] = jnp.zeros(square.shape, square.dtype)
    for g in range(groups // 2):
        ends = SUBLANES * (g + 1)
        last = groups - 1 - g
        square[SUBLANES * g : ends, :] = tiles[full + g]
        square[SUBLANES * last : SUBLANES * (last + 1), :] = pltpu.roll(tiles[full + g], LANES - ends, 1)
    mirrored = square[...].T
    left = [
        jnp.where(
            lane < SUBLANES * (g + 1),
            square[SUBLANES * g : SUBLANES * (g + 1), :],
            mirrored[SUBLANES * g : SUBLANES * (g + 1), :],
        )
        for g in range(groups)
    ]
    right = [jnp.where(lane == sub + SUBLANES * g, 1.0, 0.0) for g in range(groups)]

    def row_of(value, t):
        return jnp.broadcast_to(value[t : t + 1, :], tile)

    for b in range(groups):
        first = SUBLANES * b
        columns = [
            [jnp.broadcast_to(left[g][:, first + t : first + t + 1], tile) for g in range(b, groups)]
            for t in range(SUBLANES)
        ]
        diagonal = jnp.ones(tile, jnp.float32)
        for t in range(SUBLANES):
            pivot = row_of(columns[t][0], t)
            diagonal = jnp.where(sub == t, pivot, diagonal)
            part = 1.0 / pivot
            row_left = row_of(left[b], t) * part
            row_right = row_of(right[b], t) * part
            rest = range(t + 1, SUBLANES)
            row_columns = [row_of(columns[s][0], t) * part for s in rest]
            for g in range(b, groups):
                weight = columns[t][g - b]
                if g == b:
                    weight = jnp.where(sub > t, weight, 0.0)
                left[g] = left[g] - weight * row_left
                right[g] = right[g] - weight * row_right
                for s, row_column in zip(rest, row_columns):
                    columns[s][g - b] = columns[s][g - b] - weight * row_column
        inverse[first : first + SUBLANES, :] = (right[b] * lax.rsqrt(diagonal))[:, :size]

    contract = (((1,), (1,)), ((), ()))
    exact = dict(precision=lax.Precision.HIGHEST, preferred_element_type=jnp.float32)
    half = lax.dot_general(inverse[...], crossed[...], contract, **exact)
    result[...] = lax.dot_general(half, inverse[...], contract, **exact)
    write = pltpu.make_async_copy(result, projected, written)
    write.start()

    rotation = inverse[...].astype(jnp.bfloat16)
    product = jnp.dot(rotation, filtered[...], preferred_element_type=jnp.float32) * scale
    width = turned.shape[3]
    for row in range(rows):
        staged[pl.ds(row, size, stride=rows), :] = product[:, row * width : (row + 1) * width]
    turned[...] = staged[...].reshape(turned.shape).astype(turned.dtype)
    write.wait()


def projected_and_turned(whole, filtered, scale, peers, rows):
    size = filtered.shape[0]
    width = filtered.shape[1] // rows
    vmem = pl.BlockSpec(memory_space=pltpu.VMEM)
    matrix = pltpu.VMEM((size, size), jnp.float32)
    return pl.pallas_call(
        functools.partial(turn_kernel, scale),
        out_shape=(
            jax.ShapeDtypeStruct((size, size), jnp.float32),
            jax.ShapeDtypeStruct((peers, size // peers, rows, width), jnp.bfloat16),
        ),
        in_specs=[vmem, vmem],
        out_specs=(pl.BlockSpec(memory_space=pl.ANY), vmem),
        scratch_shapes=[
            matrix,
            matrix,
            matrix,
            pltpu.VMEM((size * rows, width), jnp.float32),
            pltpu.VMEM((LANES, LANES), jnp.float32),
            pltpu.SemaphoreType.DMA,
        ],
        compiler_params=pltpu.CompilerParams(vmem_limit_bytes=8 * 1024 * 1024),
        name="projected_and_turned",
    )(whole, filtered)


def per_device(initial_block, labels, filter_low, filter_high):
    share, _, height, width = initial_block.shape
    group, blocks = lax.axis_size(GROUP), lax.axis_size(MODE)
    local = share // group
    modes = share * blocks
    rows = height // blocks
    scale = math.sqrt(height * width * group * lax.axis_size("z"))

    own = lax.all_to_all(packed(initial_block, labels, group), GROUP, 0, 0, tiled=True)
    extra = REACH - group
    lo, hi = shifted(own, "z", 1), shifted(own, "z", -1)
    far_lo, far_hi = shifted(own[group - extra :], "z", 2), shifted(own[:extra], "z", -2)

    lowest, highest = filter_low, filter_high
    pair = filtered_and_applied(lowest, highest, far_lo, lo, own, hi, far_hi, blocks)
    pair = pair.reshape(blocks * group, 2 * local, rows, width)

    pair = lax.all_to_all(pair, LAYER, 0, 0, tiled=True)
    filtered = pair[:, :local].reshape(modes, rows * width)
    applied = pair[:, local:].reshape(modes, rows * width)
    total = total_over_all(packed_terms(filtered, applied, blocks * group))
    projected, turned = projected_and_turned(total, filtered, scale, blocks, rows)
    turned = lax.all_to_all(turned, MODE, 0, 0, tiled=True)
    modes_out = jnp.transpose(turned, (1, 0, 2, 3)).reshape(share, 1, height, width)
    return (modes_out, projected)


def solution(mesh):
    devices = mesh.devices
    slabs, modes = devices.shape
    fine = Mesh(devices.reshape(slabs // 4, 2, 2, 2, modes // 2), AXES)
    placed = (P(MODE, ("z",) + GROUP, None, None), P(("z",) + GROUP, None, None), P(), P())
    return jax.shard_map(
        per_device,
        mesh=fine,
        in_specs=placed,
        out_specs=(P(MODE, ("z",) + GROUP, None, None), P()),
        check_vma=False,
    )
```

```python
import functools
import math

import jax
import jax.numpy as jnp
from jax import lax
from jax.experimental import pallas as pl
from jax.experimental.pallas import tpu as pltpu
from jax.sharding import Mesh, PartitionSpec as P

DEGREE = 4
ROOTS = (0.0, 0.7745967, 1.0, 1.3416408)
REACH = DEGREE + 1
SUBLANES, LANES = 8, 128
UNROLL = 6

AXES = ("z", "xl", "core", "xh", "y")
GROUP = ("xl", "core")
MODE = ("xh", "y")
LAYER = ("xh", "y", "xl", "core")


def root_of(label):
    root = jnp.where(label == 1.0, ROOTS[1], 0.0)
    root = jnp.where(label == 2.0, ROOTS[2], root)
    return jnp.where(label == 3.0, ROOTS[3], root)


def inverse_root_of(label):
    value = jnp.where(label == 1.0, 1.0 / ROOTS[1], 0.0)
    value = jnp.where(label == 2.0, 1.0 / ROOTS[2], value)
    return jnp.where(label == 3.0, 1.0 / ROOTS[3], value)


def filter_kernel(lowest, highest, lo, own, hi, out, short, share, even, odd, strong, square, degree):
    planes, height, width = degree.shape
    local = even.shape[1]
    rows = out.shape[3]
    depth = own.shape[0]
    low, high = lowest[...], highest[...]
    centre = 0.5 * (high + low)
    scale = 1.0 / (0.5 * (high - low))
    inner = pl.ds(SUBLANES, height)
    lane = lax.broadcasted_iota(jnp.int32, (height, width), 1)

    def beside(ref, plane, *index):
        value = ref[(plane, *index, inner)]
        up = ref[(plane, *index, pl.ds(SUBLANES - 1, height))]
        down = ref[(plane, *index, pl.ds(SUBLANES + 1, height))]
        left = jnp.where(lane == 0, 0.0, pltpu.roll(value, 1, 1))
        right = jnp.where(lane == width - 1, 0.0, pltpu.roll(value, width - 1, 1))
        before, after = ref[(plane - 1, *index, inner)], ref[(plane + 1, *index, inner)]
        return value, (up + down) + (left + right) + (before + after)

    edge = jnp.zeros((SUBLANES, width), jnp.float32)

    def clear(plane, carry):
        for first in (0, SUBLANES + height):
            strong[plane, pl.ds(first, SUBLANES)] = edge
            for mode in range(local):
                even[plane, mode, pl.ds(first, SUBLANES)] = edge
                odd[plane, mode, pl.ds(first, SUBLANES)] = edge
        return carry

    lax.fori_loop(0, planes, clear, 0, unroll=planes // 2)

    for plane in (0, planes - 1):
        strong[plane, inner] = jnp.zeros((height, width), jnp.float32)
        for mode in range(local):
            even[plane, mode, inner] = jnp.zeros((height, width), jnp.float32)

    for source, start in ((lo, REACH - depth), (own, REACH), (hi, REACH + depth)):

        def load(index, carry, source=source, start=start):
            root = root_of(source[index, local].astype(jnp.float32))
            strong[start + index, inner] = root
            square[start + index] = root * root
            for mode in range(local):
                even[start + index, mode, inner] = root * source[index, mode].astype(jnp.float32)
            return carry

        lax.fori_loop(0, depth, load, 0, unroll=min(depth, UNROLL))

    def weigh(plane, carry):
        root, around = beside(strong, plane)
        degree[plane] = root * around
        return carry

    lax.fori_loop(1, planes - 1, weigh, 0, unroll=UNROLL)

    cur, prev = even, odd
    for step in range(DEGREE):
        factor = scale if step == 0 else 2.0 * scale

        def advance(plane, carry, cur=cur, prev=prev, factor=factor, step=step):
            here = (degree[plane] - centre) * factor
            there = square[plane] * factor
            for mode in range(local):
                value, around = beside(cur, plane, mode)
                value = here * value - there * around
                if step > 0:
                    value = value - prev[plane, mode, inner]
                prev[plane, mode, inner] = value
            return carry

        lax.fori_loop(step + 1, planes - step - 1, advance, 0, unroll=UNROLL)
        cur, prev = prev, cur

    for index in range(depth):
        plane = REACH + index
        heavy, weight = degree[plane], square[plane]
        upright = inverse_root_of(own[index, local].astype(jnp.float32))
        for mode in range(local):
            value, around = beside(cur, plane, mode)
            image = upright * (heavy * value - weight * around)
            out[:, index, mode] = (upright * value).reshape(-1, rows, width).astype(out.dtype)
            if index == 0:
                short[0, mode] = image
            elif index == depth - 1:
                short[1, mode] = image
            else:
                out[:, index, local + mode] = image.reshape(-1, rows, width).astype(out.dtype)

    for side, (outer, step) in enumerate(((REACH - depth, 1), (planes - 1 - REACH + depth, -1))):
        between = square[outer]
        for index in range(1, DEGREE):
            between = between * square[outer + step * index]
        share[side] = (8.0 * scale * scale * scale * scale) * between * strong[outer + step * DEGREE, inner]


def finish_kernel(lo, hi, far_lo, far_hi, short, share, done, out):
    out[...] = done[...]
    local = short.shape[1]
    depth, rows, width = out.shape[1], out.shape[3], out.shape[4]
    sides = ((lo, 0, far_lo, 0, 0), (hi, depth - 1, far_hi, 0, depth - 1))
    for side, (near, near_plane, far, far_plane, index) in enumerate(sides):
        weight = share[side] * root_of(far[far_plane, local].astype(jnp.float32))
        for mode in range(local):
            jump = near[near_plane, mode].astype(jnp.float32) - far[far_plane, mode].astype(jnp.float32)
            image = short[side, mode] + weight * jump
            out[:, index, local + mode] = image.reshape(-1, rows, width).astype(out.dtype)


def filtered_and_applied(lowest, highest, far_lo, lo, own, hi, far_hi, blocks):
    depth, fields, height, width = own.shape
    local = fields - 1
    planes = depth + 2 * REACH
    rimmed = pltpu.VMEM((planes, local, height + 2 * SUBLANES, width), jnp.float32)
    root = pltpu.VMEM((planes, height + 2 * SUBLANES, width), jnp.float32)
    flat = pltpu.VMEM((planes, height, width), jnp.float32)
    vmem = pl.BlockSpec(memory_space=pltpu.VMEM)
    whole = jax.ShapeDtypeStruct((blocks, depth, 2 * local, height // blocks, width), jnp.bfloat16)
    steps = planes * local * height * width
    whole_part, short, share = pl.pallas_call(
        filter_kernel,
        out_shape=(
            whole,
            jax.ShapeDtypeStruct((2, local, height, width), jnp.float32),
            jax.ShapeDtypeStruct((2, height, width), jnp.float32),
        ),
        in_specs=[pl.BlockSpec(memory_space=pltpu.SMEM)] * 2 + [vmem] * 3,
        out_specs=(vmem,) * 3,
        scratch_shapes=[rimmed, rimmed, root, flat, flat],
        compiler_params=pltpu.CompilerParams(vmem_limit_bytes=40 * 1024 * 1024),
        cost_estimate=pl.CostEstimate(flops=100 * steps, bytes_accessed=8 * steps, transcendentals=0),
        name="chebyshev_filter",
    )(lowest, highest, lo, own, hi)
    return pl.pallas_call(
        finish_kernel,
        out_shape=whole,
        in_specs=[vmem] * 7,
        out_specs=vmem,
        compiler_params=pltpu.CompilerParams(vmem_limit_bytes=8 * 1024 * 1024),
        name="outermost_planes",
    )(lo, hi, far_lo, far_hi, short, share, whole_part)


def pack_kernel(block, labels, out):
    group, fields = out.shape[:2]
    local = fields - 1
    tags = labels[0].astype(jnp.float32).astype(out.dtype)
    for peer in range(group):
        for mode in range(local):
            out[peer, mode] = block[peer * local + mode, 0]
        out[peer, local] = tags


def packed(block, labels, group):
    share, _, height, width = block.shape
    vmem = pl.BlockSpec(memory_space=pltpu.VMEM)
    return pl.pallas_call(
        pack_kernel,
        out_shape=jax.ShapeDtypeStruct((group, share // group + 1, height, width), block.dtype),
        in_specs=[vmem, vmem],
        out_specs=vmem,
        compiler_params=pltpu.CompilerParams(vmem_limit_bytes=8 * 1024 * 1024),
        name="pack",
    )(block, labels)


def shifted(value, axis, step):
    size = lax.axis_size(axis)
    pairs = [(i, i + step) for i in range(size) if 0 <= i + step < size]
    return lax.ppermute(value, axis, pairs)


def summed_over_z(value):
    copies = jnp.broadcast_to(value, (lax.axis_size("z"),) + value.shape)
    return jnp.sum(lax.all_to_all(copies, "z", 0, 0, tiled=True), axis=0)


def lanes_of():
    return lax.broadcasted_iota(jnp.int32, (SUBLANES, LANES), 1)


def gram_kernel(filtered, applied, out, wide):
    size = filtered.shape[0]
    groups = size // SUBLANES
    spare = LANES - size
    full = groups - groups * spare // LANES
    lane = lanes_of()
    wide[...] = jnp.zeros(wide.shape, wide.dtype)
    contract = (((1,), (1,)), ((), ()))
    for half, source in enumerate((applied, filtered)):
        product = lax.dot_general(source[...], filtered[...], contract, preferred_element_type=jnp.float32)
        wide[half * size : (half + 1) * size, :size] = product

    def group_of(half, g):
        return wide[half * size + SUBLANES * g : half * size + SUBLANES * (g + 1), :]

    pieces = size // spare
    tiles = []
    for t in range(full):
        extra = group_of(0, full + t // pieces)
        tiles.append(jnp.where(lane < size, group_of(0, t), pltpu.roll(extra, size - spare * (t % pieces), 1)))
    for g in range(groups // 2):
        ends = SUBLANES * (g + 1)
        tiles.append(jnp.where(lane < ends, group_of(1, g), pltpu.roll(group_of(1, groups - 1 - g), ends, 1)))
    half_rows = out.shape[1]
    for t, tile in enumerate(tiles):
        out[2 * t] = tile[:half_rows]
        out[2 * t + 1] = tile[half_rows:]
    for rest in range(2 * len(tiles), out.shape[0]):
        out[rest] = jnp.zeros(out.shape[1:], out.dtype)


def packed_terms(filtered, applied, peers):
    size = filtered.shape[0]
    vmem = pl.BlockSpec(memory_space=pltpu.VMEM)
    return pl.pallas_call(
        gram_kernel,
        out_shape=jax.ShapeDtypeStruct((peers, SUBLANES // 2, LANES), jnp.float32),
        in_specs=[vmem, vmem],
        out_specs=vmem,
        scratch_shapes=[pltpu.VMEM((2 * size, LANES), jnp.float32)],
        compiler_params=pltpu.CompilerParams(vmem_limit_bytes=8 * 1024 * 1024),
        name="packed_terms",
    )(filtered, applied)


def total_over_all(partial):
    terms = lax.all_to_all(partial, LAYER, 0, 0, tiled=True)
    mine = summed_over_z(jnp.sum(terms, axis=0))
    return lax.all_to_all(jnp.broadcast_to(mine, partial.shape), LAYER, 0, 0, tiled=True)


def turn_kernel(scale, whole, filtered, projected, turned, inverse, crossed, result, staged, square, written):
    size = inverse.shape[0]
    rows = turned.shape[2]
    groups = size // SUBLANES
    spare = LANES - size
    full = groups - groups * spare // LANES
    pieces = size // spare
    tile = (SUBLANES, LANES)
    sub = lax.broadcasted_iota(jnp.int32, tile, 0)
    lane = lanes_of()
    tiles = [jnp.concatenate([whole[2 * t], whole[2 * t + 1]], axis=0) for t in range(full + groups // 2)]

    for g in range(full):
        crossed[SUBLANES * g : SUBLANES * (g + 1), :] = tiles[g][:, :size]
    for g in range(full, groups):
        first = pieces * (g - full)
        value = pltpu.roll(tiles[first], spare, 1)
        for p in range(1, pieces):
            value = jnp.where(lane < spare * p, value, pltpu.roll(tiles[first + p], spare * (p + 1), 1))
        crossed[SUBLANES * g : SUBLANES * (g + 1), :] = value[:, :size]

    square[...] = jnp.zeros(square.shape, square.dtype)
    for g in range(groups // 2):
        ends = SUBLANES * (g + 1)
        last = groups - 1 - g
        square[SUBLANES * g : ends, :] = tiles[full + g]
        square[SUBLANES * last : SUBLANES * (last + 1), :] = pltpu.roll(tiles[full + g], LANES - ends, 1)
    mirrored = square[...].T
    left = [
        jnp.where(
            lane < SUBLANES * (g + 1),
            square[SUBLANES * g : SUBLANES * (g + 1), :],
            mirrored[SUBLANES * g : SUBLANES * (g + 1), :],
        )
        for g in range(groups)
    ]
    right = [jnp.where(lane == sub + SUBLANES * g, 1.0, 0.0) for g in range(groups)]

    def row_of(value, t):
        return jnp.broadcast_to(value[t : t + 1, :], tile)

    for b in range(groups):
        first = SUBLANES * b
        columns = [
            [jnp.broadcast_to(left[g][:, first + t : first + t + 1], tile) for g in range(b, groups)]
            for t in range(SUBLANES)
        ]
        diagonal = jnp.ones(tile, jnp.float32)
        for t in range(SUBLANES):
            pivot = row_of(columns[t][0], t)
            diagonal = jnp.where(sub == t, pivot, diagonal)
            part = 1.0 / pivot
            row_left = row_of(left[b], t) * part
            row_right = row_of(right[b], t) * part
            rest = range(t + 1, SUBLANES)
            row_columns = [row_of(columns[s][0], t) * part for s in rest]
            for g in range(b, groups):
                weight = columns[t][g - b]
                if g == b:
                    weight = jnp.where(sub > t, weight, 0.0)
                left[g] = left[g] - weight * row_left
                right[g] = right[g] - weight * row_right
                for s, row_column in zip(rest, row_columns):
                    columns[s][g - b] = columns[s][g - b] - weight * row_column
        inverse[first : first + SUBLANES, :] = (right[b] * lax.rsqrt(diagonal))[:, :size]

    contract = (((1,), (1,)), ((), ()))
    exact = dict(precision=lax.Precision.HIGHEST, preferred_element_type=jnp.float32)
    half = lax.dot_general(inverse[...], crossed[...], contract, **exact)
    result[...] = lax.dot_general(half, inverse[...], contract, **exact)
    write = pltpu.make_async_copy(result, projected, written)
    write.start()

    rotation = inverse[...].astype(jnp.bfloat16)
    product = jnp.dot(rotation, filtered[...], preferred_element_type=jnp.float32) * scale
    width = turned.shape[3]
    for row in range(rows):
        staged[pl.ds(row, size, stride=rows), :] = product[:, row * width : (row + 1) * width]
    turned[...] = staged[...].reshape(turned.shape).astype(turned.dtype)
    write.wait()


def projected_and_turned(whole, filtered, scale, peers, rows):
    size = filtered.shape[0]
    width = filtered.shape[1] // rows
    vmem = pl.BlockSpec(memory_space=pltpu.VMEM)
    matrix = pltpu.VMEM((size, size), jnp.float32)
    return pl.pallas_call(
        functools.partial(turn_kernel, scale),
        out_shape=(
            jax.ShapeDtypeStruct((size, size), jnp.float32),
            jax.ShapeDtypeStruct((peers, size // peers, rows, width), jnp.bfloat16),
        ),
        in_specs=[vmem, vmem],
        out_specs=(pl.BlockSpec(memory_space=pl.ANY), vmem),
        scratch_shapes=[
            matrix,
            matrix,
            matrix,
            pltpu.VMEM((size * rows, width), jnp.float32),
            pltpu.VMEM((LANES, LANES), jnp.float32),
            pltpu.SemaphoreType.DMA,
        ],
        compiler_params=pltpu.CompilerParams(vmem_limit_bytes=8 * 1024 * 1024),
        name="projected_and_turned",
    )(whole, filtered)


def per_device(initial_block, labels, filter_low, filter_high):
    share, _, height, width = initial_block.shape
    group, blocks = lax.axis_size(GROUP), lax.axis_size(MODE)
    local = share // group
    modes = share * blocks
    rows = height // blocks
    scale = math.sqrt(height * width * group * lax.axis_size("z"))

    own = lax.all_to_all(packed(initial_block, labels, group), GROUP, 0, 0, tiled=True)
    extra = REACH - group
    lo, hi = shifted(own, "z", 1), shifted(own, "z", -1)
    far_lo, far_hi = shifted(own[group - extra :], "z", 2), shifted(own[:extra], "z", -2)

    lowest, highest = filter_low, filter_high
    pair = filtered_and_applied(lowest, highest, far_lo, lo, own, hi, far_hi, blocks)
    pair = pair.reshape(blocks * group, 2 * local * rows, width)

    pair = lax.all_to_all(pair, LAYER, 0, 0, tiled=True).reshape(blocks * group, 2 * local, rows, width)
    filtered = pair[:, :local].reshape(modes, rows * width)
    applied = pair[:, local:].reshape(modes, rows * width)
    total = total_over_all(packed_terms(filtered, applied, blocks * group))
    projected, turned = projected_and_turned(total, filtered, scale, blocks, rows)
    turned = lax.all_to_all(turned, MODE, 0, 0, tiled=True)
    modes_out = jnp.transpose(turned, (1, 0, 2, 3)).reshape(share, 1, height, width)
    return (modes_out, projected)


def solution(mesh):
    devices = mesh.devices
    slabs, modes = devices.shape
    fine = Mesh(devices.reshape(slabs // 4, 2, 2, 2, modes // 2), AXES)
    placed = (P(MODE, ("z",) + GROUP, None, None), P(("z",) + GROUP, None, None), P(), P())
    return jax.shard_map(
        per_device,
        mesh=fine,
        in_specs=placed,
        out_specs=(P(MODE, ("z",) + GROUP, None, None), P()),
        check_vma=False,
    )
```
